512 devices in a mesh: rows: 64 (over z, x), grp: 8 (over y, core).
Axes of the slice: x: 4, y: 4, z: 16, core: 2. Of those that a mesh axis runs over, the one named last changes fastest.
Arguments:
- panel: bfloat16 [131072, 256], P(('rows', 'grp')), may hold values from -6 to 6
- tile_lists: int32 [3, 32768], P(None, ('rows', 'grp')), may hold values from 0 to 15, as said below
- tile_values: float32 [32768, 128, 128], P(('rows', 'grp')), may hold values from -0.0625 to 0.0625
Outputs:
- basis: float32 [131072, 256], P(('rows', 'grp'))
The draws below stay inside these ranges and needn't reach their ends.
Inputs may be any that keep to these rules, and one draw needn't show every extreme that they name: `tile_lists`: A slot facing row group s on a device of row group r is live only if s >= r; the slot with s = r is always live, and its column block is not before its row block. Row entries lie below 2; flags are 0 or 1.
All inputs are finite; a program needn't handle non-finite values.
Results may differ from the reference program's by a relative error of at most 0.0003.
Values may be sent and summed in bfloat16 or wider, within the bound.
A program may use at most 128 MiB of HBM per device.

```python
import jax
import jax.numpy as jnp
from jax import lax

TILE = 128
PANEL = 256
ROWS_DEV = 256
SLOTS = 64
NODES = 131072
N_ROWS = 64
N_GRP = 8
DEVICES = 512


def draw_tile_lists(key, part):
    key = jax.random.fold_in(key, 11)
    keys = jax.random.split(key, 4)
    blocks = ROWS_DEV // TILE
    span = N_GRP * blocks
    devices = N_ROWS * N_GRP
    count = SLOTS * devices
    flat = jnp.arange(count, dtype=jnp.int32)
    device = flat // SLOTS
    slot = flat % SLOTS
    row_group = device // N_GRP
    member = device % N_GRP
    row_local = jax.random.randint(keys[0], (count,), 0, blocks, dtype=jnp.int32)
    own_index = member * blocks + row_local
    col_any = jax.random.randint(keys[1], (count,), 0, span, dtype=jnp.int32)
    col_upper = jax.random.randint(keys[2], (count,), own_index, span, dtype=jnp.int32)
    col_local = jnp.where(slot == row_group, col_upper, col_any)
    coin = jax.random.randint(keys[3], (count,), 0, 4, dtype=jnp.int32)
    live = jnp.where(slot == row_group, 1, jnp.where((slot > row_group) & (coin < 3), 1, 0))
    return jnp.stack([row_local, col_local, live.astype(jnp.int32)]).astype(jnp.int32)


def block_levels(key, extent, shards, low, top_value):
    loudness, own = 1.0, jax.random.fold_in(key, 6)
    for dim, parts in shards:
        heights = jnp.exp(jax.random.uniform(jax.random.fold_in(own, dim), (parts,), jnp.float32, low / len(shards), top_value / len(shards)))
        loudness = loudness * jnp.repeat(heights, extent[dim] // parts).reshape([-1 if axis == dim else 1 for axis in range(len(extent))])
    return loudness


def normal_values(stream_key, dims, scale, most, pieces=(), kind=jnp.bfloat16):
    drawn = jax.random.normal(stream_key, dims, jnp.float32) * scale
    if len(pieces) > 0:
        drawn = block_levels(stream_key, dims, pieces, -0.22, 0.18) * drawn
    return jnp.clip(drawn, min=-most, max=most).astype(kind)


def setup_inputs(seed: int = 0) -> dict:
    splits = jax.random.split(jax.random.key(seed), 4)
    panel = normal_values(splits[0], (NODES, PANEL), 1.0, 6.0, ((0, 512),))
    tile_lists = draw_tile_lists(jax.random.fold_in(splits[3], 71), 0)
    tile_values = normal_values(splits[2], (SLOTS * DEVICES, TILE, TILE), (TILE * SLOTS) ** -0.5, 0.0625, ((0, 512),), jnp.float32)
    return {"panel": panel, "tile_lists": tile_lists, "tile_values": tile_values}


def reference(panel, tile_lists, tile_values):
    blocks = ROWS_DEV // TILE
    span = N_GRP * blocks
    devices = N_ROWS * N_GRP
    total_blocks = NODES // TILE
    qblocks = panel.astype(jnp.float32).reshape(total_blocks, TILE, PANEL)
    lists = tile_lists.reshape(3, devices, SLOTS).transpose(1, 0, 2)
    values = tile_values.reshape(devices, SLOTS, TILE, TILE)
    device_ids = jnp.arange(devices, dtype=jnp.int32)

    def visit(accum, inputs):
        entry, vals, dev = inputs
        live = entry[2].astype(jnp.float32)
        masked = vals * live[:, None, None]
        row_glob = (dev * blocks + entry[0]).astype(jnp.int32)
        col_glob = (jnp.arange(SLOTS, dtype=jnp.int32) * span + entry[1]).astype(jnp.int32)
        forward = jnp.einsum('sij,sjk->sik', masked, qblocks[col_glob], precision=lax.Precision.HIGHEST)
        backward = jnp.einsum('sji,sjk->sik', masked, qblocks[row_glob], precision=lax.Precision.HIGHEST)
        accum = accum.at[row_glob].add(forward)
        accum = accum.at[col_glob].add(backward)
        return (accum, None)
    start = jnp.zeros((total_blocks, TILE, PANEL), jnp.float32)
    product, _ = lax.scan(visit, start, (lists, values, device_ids))
    product = product.reshape(NODES, PANEL)
    gram = jnp.dot(product.T, product, precision=lax.Precision.HIGHEST) / NODES
    lower = jnp.linalg.cholesky(gram)
    solved = jax.scipy.linalg.solve_triangular(lower, product.T, lower=True)
    return solved.T
```

```python
import functools

import jax
import jax.numpy as jnp
from jax import lax
from jax.experimental import pallas as pl
from jax.experimental.pallas import tpu as pltpu
from jax.sharding import Mesh, PartitionSpec as P

HIGHEST = lax.Precision.HIGHEST
MESH = pl.DeviceIdType.MESH
VMEM_LIMIT = 56 * 1024 * 1024
AXES = ("z", "x", "y", "core")
PLANE = ("x", "y", "core")
GROUP = ("y", "core")


def axis_sizes():
    return tuple(lax.axis_size(a) for a in AXES)


def split2(t):
    high = t.astype(jnp.bfloat16)
    low = (t - high.astype(jnp.float32)).astype(jnp.bfloat16)
    return high, low


def tiles_kernel(his, blocks, span, step, meta, tiles, cols, rows, fwd, bwd):
    at = pl.program_id(0)

    @pl.when(at == 0)
    def _():
        bwd[...] = jnp.zeros_like(bwd)

    for u in range(step):
        src = at * step + u
        values, panels, picks = [], [], []
        for hi in range(his):
            slot = src * his + hi
            row, col, live = meta[0, slot], meta[1, slot], meta[2, slot]
            t = tiles[u, hi] * live.astype(jnp.float32)
            values.append(t)
            picks.append(row)
            panels.append(cols[(col // blocks), hi, col % blocks])
            flipped = jnp.concatenate(split2(t.T), axis=1)
            own = rows[u, row]
            got = jnp.dot(
                flipped, jnp.concatenate([own, own], axis=0), preferred_element_type=jnp.float32
            )
            bwd[hi, col] += got
        left = jnp.concatenate(
            [
                jnp.concatenate(
                    [t * (pick == b).astype(jnp.float32) for t, pick in zip(values, picks)], axis=1
                )
                for b in range(blocks)
            ],
            axis=0,
        )
        right = jnp.concatenate(panels, axis=0)
        high, low = split2(left)
        out = jnp.dot(high, right, preferred_element_type=jnp.float32) + jnp.dot(
            low, right, preferred_element_type=jnp.float32
        )
        fwd[u] = out.reshape(fwd.shape[1:])


def tile_products(meta, tiles, cols, rows):
    plane, his, tile, _ = tiles.shape
    blocks, width = rows.shape[1], rows.shape[3]
    span = cols.shape[0] * blocks
    step = 4
    return pl.pallas_call(
        functools.partial(tiles_kernel, his, blocks, span, step),
        grid_spec=pltpu.PrefetchScalarGridSpec(
            num_scalar_prefetch=1,
            grid=(plane // step,),
            in_specs=[
                pl.BlockSpec((step, his, tile, tile), lambda i, m: (i, 0, 0, 0)),
                pl.BlockSpec(cols.shape, lambda i, m: (0, 0, 0, 0, 0)),
                pl.BlockSpec((step, blocks, tile, width), lambda i, m: (i, 0, 0, 0)),
            ],
            out_specs=[
                pl.BlockSpec((step, blocks, tile, width), lambda i, m: (i, 0, 0, 0)),
                pl.BlockSpec((his, span, tile, width), lambda i, m: (0, 0, 0, 0)),
            ],
        ),
        out_shape=[
            jax.ShapeDtypeStruct((plane, blocks, tile, width), jnp.float32),
            jax.ShapeDtypeStruct((his, span, tile, width), jnp.float32),
        ],
        compiler_params=pltpu.CompilerParams(vmem_limit_bytes=VMEM_LIMIT),
        name="tile_products",
    )(meta, tiles, cols, rows)


def gram_kernel(sizes, first, second, product, gram, part, got, ring, whole, sent, came):
    nz, nx, ny, nc = sizes
    plane = nx * ny * nc
    group = ny * nc
    z, x, y, c = (lax.axis_index(a) for a in AXES)
    me = x * group + y * nc + c
    strip = part.shape[0] // plane

    def plane_peer(k):
        p = lax.rem(me + k, plane)
        return p, (z, p // group, lax.rem(p, group) // nc, lax.rem(p, nc))

    def ring_peer(k):
        q = lax.rem(z + k, nz)
        return q, (q, x, y, c)

    barrier = pltpu.get_barrier_semaphore()

    def greet(peer):
        def body(k, carry):
            pl.semaphore_signal(barrier, inc=1, device_id=peer(k)[1], device_id_type=MESH)
            return carry

        return body

    lax.fori_loop(1, plane, greet(plane_peer), 0)
    lax.fori_loop(1, nz, greet(ring_peer), 0)

    total = first[...] + second[...]
    product[...] = total
    part[...] = lax.dot_general(
        total, total, (((0,), (0,)), ((), ())), precision=HIGHEST, preferred_element_type=jnp.float32
    )
    pl.semaphore_wait(barrier, plane - 1 + nz - 1)

    def rows_of(p):
        return pl.ds(pl.multiple_of(p * strip, strip), strip)

    def exchange(count, peer, stage, mine, source, target):
        def copy(k, slot_of_source, slot_of_target, device):
            return pltpu.make_async_remote_copy(
                src_ref=slot_of_source,
                dst_ref=slot_of_target,
                send_sem=sent.at[stage, k],
                recv_sem=came.at[stage, mine],
                device_id=device,
                device_id_type=MESH,
            )

        def start(k, carry):
            p, device = peer(k)
            copy(k, source(p), target(mine), device).start()
            return carry

        def finish(k, carry):
            p, device = peer(k)
            copy(k, source(p), target(mine), device).wait_send()
            pltpu.make_async_remote_copy(
                src_ref=target(p),
                dst_ref=target(p),
                send_sem=sent.at[stage, k],
                recv_sem=came.at[stage, p],
                device_id=device,
                device_id_type=MESH,
            ).wait_recv()
            return carry

        lax.fori_loop(1, count, start, 0)
        lax.fori_loop(1, count, finish, 0)

    exchange(plane, plane_peer, 0, me, lambda p: part.at[rows_of(p)], lambda p: got.at[p])
    strip_sum = part[rows_of(me)]
    for k in range(1, plane):
        strip_sum = strip_sum + got[lax.rem(me + k, plane)]
    ring[z] = strip_sum
    exchange(nz, ring_peer, 1, z, lambda p: ring.at[z], lambda p: ring.at[p])
    strip_sum = ring[0]
    for k in range(1, nz):
        strip_sum = strip_sum + ring[k]
    whole[rows_of(me)] = strip_sum
    exchange(
        plane, plane_peer, 2, me, lambda p: whole.at[rows_of(me)], lambda p: whole.at[rows_of(p)]
    )
    gram[...] = whole[...]


def gram_sum(first, second):
    sizes = axis_sizes()
    plane = sizes[1] * sizes[2] * sizes[3]
    rows, width = first.shape
    strip = width // plane
    most = max(plane, sizes[0])
    vmem = pl.BlockSpec(memory_space=pltpu.VMEM)
    return pl.pallas_call(
        functools.partial(gram_kernel, sizes),
        out_shape=[
            jax.ShapeDtypeStruct((rows, width), jnp.float32),
            jax.ShapeDtypeStruct((width, width), jnp.float32),
        ],
        in_specs=[vmem, vmem],
        out_specs=[vmem, vmem],
        scratch_shapes=[
            pltpu.VMEM((width, width), jnp.float32),
            pltpu.VMEM((plane, strip, width), jnp.float32),
            pltpu.VMEM((sizes[0], strip, width), jnp.float32),
            pltpu.VMEM((width, width), jnp.float32),
            pltpu.SemaphoreType.DMA((3, most)),
            pltpu.SemaphoreType.DMA((3, most)),
        ],
        compiler_params=pltpu.CompilerParams(
            collective_id=0, has_side_effects=True, vmem_limit_bytes=VMEM_LIMIT
        ),
        name="gram_sum",
    )(first, second)


def dot_high(a, b, dims):
    return lax.dot_general(
        a, b, (dims, ((), ())), precision=HIGHEST, preferred_element_type=jnp.float32
    )


def inverse_factor(a):
    n = a.shape[0]
    sub = 8
    lanes = lax.broadcasted_iota(jnp.int32, (sub, n), 1)
    subs = lax.broadcasted_iota(jnp.int32, (sub, n), 0)
    left = [a[i * sub : (i + 1) * sub] for i in range(n // sub)]
    right = [(lanes == subs + i * sub).astype(jnp.float32) for i in range(n // sub)]
    for j in range(n):
        t0, s = divmod(j, sub)
        row = left[t0][s : s + 1]
        inv = 1.0 / row[:, j : j + 1]
        wrow = right[t0][s : s + 1]
        scaled = row * inv
        wscaled = wrow * inv
        for t in range(t0, n // sub):
            col = left[t][:, j : j + 1]
            if t == t0:
                col = jnp.where(subs[:, :1] > s, col, 0.0)
            left[t] = left[t] - col * scaled
            right[t] = right[t] - col * wscaled
    out = []
    for t in range(n // sub):
        d = jnp.sum(jnp.where(lanes == subs + t * sub, left[t], 0.0), axis=1, keepdims=True)
        out.append(right[t] * lax.rsqrt(d))
    return jnp.concatenate(out, axis=0)


def basis_kernel(scale, gram, product, basis):
    n = gram.shape[0]
    h = n // 2
    g11 = gram[:h, :h] * scale
    g21 = gram[h:, :h] * scale
    g22 = gram[h:, h:] * scale
    w11 = inverse_factor(g11)
    l21 = dot_high(g21, w11, ((1,), (1,)))
    w22 = inverse_factor(g22 - dot_high(l21, l21, ((1,), (1,))))
    w21 = -dot_high(w22, dot_high(l21, w11, ((1,), (0,))), ((1,), (0,)))
    first = product[:, :h]
    basis[:, :h] = dot_high(first, w11, ((1,), (1,)))
    basis[:, h:] = dot_high(first, w21, ((1,), (1,))) + dot_high(
        product[:, h:], w22, ((1,), (1,))
    )


def new_basis(gram, product, nodes):
    vmem = pl.BlockSpec(memory_space=pltpu.VMEM)
    return pl.pallas_call(
        functools.partial(basis_kernel, 1.0 / nodes),
        out_shape=jax.ShapeDtypeStruct(product.shape, jnp.float32),
        in_specs=[vmem, vmem],
        out_specs=vmem,
        compiler_params=pltpu.CompilerParams(vmem_limit_bytes=VMEM_LIMIT),
        name="new_basis",
    )(gram, product)


def shards(panel, lists, tiles):
    nz, nx, ny, nc = axis_sizes()
    group = ny * nc
    plane = nx * group
    tile = tiles.shape[1]
    width = panel.shape[1]
    blocks = panel.shape[0] // tile
    nodes = panel.shape[0] * nz * plane
    his = nz // group
    sort = (2, 1, 0)
    send = tiles.reshape(his, group, nx, tile, tile).transpose(2, 1, 0, 3, 4)
    here = lax.all_to_all(
        send.reshape(plane, his, tile, tile), PLANE, split_axis=0, concat_axis=0, tiled=True
    )
    send = lists.reshape(3, his, group, nx).transpose(3, 2, 1, 0)
    meta = lax.all_to_all(
        send.reshape(plane, his, 3), PLANE, split_axis=0, concat_axis=0, tiled=True
    )
    meta = meta.reshape(plane * his, 3).T
    own = panel.reshape(blocks, tile, width)
    rows = lax.all_gather(own, PLANE, axis=0)
    column = lax.all_gather(own, "z", axis=0).reshape(his, group, blocks, tile, width)
    cols = lax.all_to_all(
        column.transpose(1, 0, 2, 3, 4), GROUP, split_axis=0, concat_axis=0, tiled=True
    )
    fwd, bwd = tile_products(meta, here, cols, rows)
    first = lax.psum_scatter(fwd, PLANE, scatter_dimension=0, tiled=True)
    send = bwd.reshape(his, group, blocks, tile, width).transpose(1, 0, 2, 3, 4)
    spread = lax.all_to_all(send, GROUP, split_axis=0, concat_axis=0, tiled=True)
    spread = spread.transpose(1, 0, 2, 3, 4).reshape(nz, blocks, tile, width)
    second = lax.psum_scatter(spread, "z", scatter_dimension=0, tiled=True)
    product, gram = gram_sum(
        first.reshape(blocks * tile, width), second.reshape(blocks * tile, width)
    )
    return new_basis(gram, product, nodes)


def solution(mesh):
    sizes = mesh.devices.shape
    nx, ny, nc = grid_of(sizes)
    fine = Mesh(mesh.devices.reshape(sizes[0] // nx, nx, ny, nc), AXES)
    return jax.shard_map(
        shards,
        mesh=fine,
        in_specs=(P(AXES, None), P(None, AXES), P(AXES, None, None)),
        out_specs=P(AXES, None),
        check_vma=False,
    )


def grid_of(sizes):
    return (4, 4, 2) if sizes == (64, 8) else (2, 1, 2)
```

```python
import functools

import jax
import jax.numpy as jnp
from jax import lax
from jax.experimental import pallas as pl
from jax.experimental.pallas import tpu as pltpu
from jax.sharding import Mesh, PartitionSpec as P

HIGHEST = lax.Precision.HIGHEST
MESH = pl.DeviceIdType.MESH
VMEM_LIMIT = 56 * 1024 * 1024
AXES = ("z", "x", "y", "core")
PLANE = ("x", "y", "core")
GROUP = ("y", "core")


def axis_sizes():
    return tuple(lax.axis_size(a) for a in AXES)


def split2(t):
    high = t.astype(jnp.bfloat16)
    low = (t - high.astype(jnp.float32)).astype(jnp.bfloat16)
    return high, low


def tiles_kernel(his, blocks, span, step, meta, tiles, cols, rows, fwd, bwd):
    at = pl.program_id(0)

    @pl.when(at == 0)
    def _():
        bwd[...] = jnp.zeros_like(bwd)

    for u in range(step):
        src = at * step + u
        values, panels, picks = [], [], []
        for hi in range(his):
            slot = src * his + hi
            row, col, live = meta[0, slot], meta[1, slot], meta[2, slot]
            t = tiles[u, hi] * live.astype(jnp.float32)
            values.append(t)
            picks.append(row)
            panels.append(cols[(col // blocks), hi, col % blocks])
            flipped = jnp.concatenate(split2(t.T), axis=1)
            own = rows[u, row]
            got = jnp.dot(
                flipped, jnp.concatenate([own, own], axis=0), preferred_element_type=jnp.float32
            )
            bwd[hi, col] += got
        left = jnp.concatenate(
            [
                jnp.concatenate(
                    [t * (pick == b).astype(jnp.float32) for t, pick in zip(values, picks)], axis=1
                )
                for b in range(blocks)
            ],
            axis=0,
        )
        right = jnp.concatenate(panels, axis=0)
        high, low = split2(left)
        out = jnp.dot(high, right, preferred_element_type=jnp.float32) + jnp.dot(
            low, right, preferred_element_type=jnp.float32
        )
        fwd[u] = out.reshape(fwd.shape[1:])


def tile_products(meta, tiles, cols, rows):
    plane, his, tile, _ = tiles.shape
    blocks, width = rows.shape[1], rows.shape[3]
    span = cols.shape[0] * blocks
    step = 4
    return pl.pallas_call(
        functools.partial(tiles_kernel, his, blocks, span, step),
        grid_spec=pltpu.PrefetchScalarGridSpec(
            num_scalar_prefetch=1,
            grid=(plane // step,),
            in_specs=[
                pl.BlockSpec((step, his, tile, tile), lambda i, m: (i, 0, 0, 0)),
                pl.BlockSpec(cols.shape, lambda i, m: (0, 0, 0, 0, 0)),
                pl.BlockSpec((step, blocks, tile, width), lambda i, m: (i, 0, 0, 0)),
            ],
            out_specs=[
                pl.BlockSpec((step, blocks, tile, width), lambda i, m: (i, 0, 0, 0)),
                pl.BlockSpec((his, span, tile, width), lambda i, m: (0, 0, 0, 0)),
            ],
        ),
        out_shape=[
            jax.ShapeDtypeStruct((plane, blocks, tile, width), jnp.float32),
            jax.ShapeDtypeStruct((his, span, tile, width), jnp.float32),
        ],
        compiler_params=pltpu.CompilerParams(vmem_limit_bytes=VMEM_LIMIT),
        name="tile_products",
    )(meta, tiles, cols, rows)


CHUNK = 64
SKEW = 2


def sums_kernel(
    sizes,
    fwd,
    bwd,
    product,
    gram,
    held,
    keep,
    from_core,
    from_x,
    from_y,
    from_below,
    from_above,
    last,
    part,
    got,
    ring,
    whole,
    local_sem,
    chain_sent,
    chain_came,
    last_sent,
    last_came,
    plane_sent,
    plane_came,
    sent,
    came,
):
    nz, nx, ny, nc = sizes
    group = ny * nc
    plane = nx * group
    half = nz // 2
    z, x, y, c = (lax.axis_index(a) for a in AXES)
    g = y * nc + c
    me = x * group + g
    strip = part.shape[0] // plane
    chunks = held.shape[1]
    per_device = last.shape[0]

    def member(p):
        return (z, x, p // nc, lax.rem(p, nc))

    def plane_peer(k):
        p = lax.rem(me + k, plane)
        return p, (z, p // group, lax.rem(p, group) // nc, lax.rem(p, nc))

    def ring_peer(k):
        q = lax.rem(z + k, nz)
        return q, (q, x, y, c)

    def remote(source, target, send_sem, recv_sem, device):
        return pltpu.make_async_remote_copy(
            src_ref=source,
            dst_ref=target,
            send_sem=send_sem,
            recv_sem=recv_sem,
            device_id=device,
            device_id_type=MESH,
        )

    barrier = pltpu.get_barrier_semaphore()

    def greet(peer):
        def body(k, carry):
            pl.semaphore_signal(barrier, inc=1, device_id=peer(k)[1], device_id_type=MESH)
            return carry

        return body

    lax.fori_loop(1, plane, greet(plane_peer), 0)
    lax.fori_loop(1, nz, greet(ring_peer), 0)
    load_held = pltpu.make_async_copy(bwd, held, local_sem.at[0])
    load_keep = pltpu.make_async_copy(fwd.at[:, c], keep, local_sem.at[1])
    load_held.start()
    load_keep.start()
    pl.semaphore_wait(barrier, plane - 1 + nz - 1)

    other = (z, x, y, nc - 1 - c)
    core_copy = remote(
        fwd.at[:, nc - 1 - c], from_core, plane_sent.at[0, 0], plane_came.at[0, 0], other
    )
    core_copy.start()

    d0 = lax.rem(g - z + nz, nz)
    lower = jnp.logical_and(d0 >= 1, d0 <= half)
    hu = jnp.where(lower, 0, 1)
    hd = 1 - hu
    du = jnp.where(lower, d0, lax.rem(d0 + half, nz))
    pu = half - du
    pd = du - 1
    target = du == half
    above = (lax.rem(z + 1, nz), x, y, c)
    below = (lax.rem(z + nz - 1, nz), x, y, c)

    def up(j):
        return remote(
            held.at[hu, j], from_below.at[j], chain_sent.at[0, j], chain_came.at[0, j], above
        )

    def down(j):
        return remote(
            held.at[hd, j], from_above.at[j], chain_sent.at[1, j], chain_came.at[1, j], below
        )

    def scatter(j, at):
        return remote(
            held.at[hd, j], last.at[at], last_sent.at[j], last_came.at[at], member(j // per_device)
        )

    load_held.wait()

    def step(i, carry):
        j = i - SKEW * pu

        @pl.when(jnp.logical_and(j >= 0, j < chunks))
        def _():
            @pl.when(pu > 0)
            def _():
                up(j).wait_recv()
                held[hu, j] += from_below[j]

            up(j).start()

        jd = i - SKEW * pd

        @pl.when(jnp.logical_and(jnp.logical_not(target), jnp.logical_and(jd >= 0, jd < chunks)))
        def _():
            @pl.when(pd > 0)
            def _():
                down(jd).wait_recv()
                held[hd, jd] += from_above[jd]

            down(jd).start()

        jt = i - SKEW * half

        @pl.when(jnp.logical_and(target, jnp.logical_and(jt >= 0, jt < chunks)))
        def _():
            up(jt).wait_recv()
            down(jt).wait_recv()
            held[hd, jt] += from_below[jt] + from_above[jt]
            at = lax.rem(jt, per_device)

            @pl.when(jt // per_device == g)
            def _():
                last[at] = held[hd, jt]

            @pl.when(jt // per_device != g)
            def _():
                scatter(jt, at).start()

        return carry

    steps = chunks + SKEW * half
    cut = (steps // 5, (3 * steps) // 4)
    lax.fori_loop(0, cut[0], step, 0)

    load_keep.wait()
    core_copy.wait()

    def x_copy(k):
        p = lax.rem(x + k, nx)
        return remote(
            keep.at[pl.ds(p * ny, ny)],
            from_x.at[x],
            plane_sent.at[1, k],
            plane_came.at[1, x],
            (z, p, y, c),
        )

    def x_source(k):
        p = lax.rem(x + k, nx)
        return p, remote(
            from_x.at[p], from_x.at[p], plane_sent.at[1, k], plane_came.at[1, p], (z, p, y, c)
        )

    for k in range(1, nx + 1):
        p = lax.rem(x + k, nx)

        def add_core(i, carry, p=p):
            keep[p * ny + i] += from_core[p * ny + i]
            return carry

        lax.fori_loop(0, ny, add_core, 0)
        if k < nx:
            x_copy(k).start()

    lax.fori_loop(cut[0], cut[1], step, 0)

    for k in range(1, nx):
        p, copy = x_source(k)
        copy.wait_recv()

        def add_x(i, carry, p=p):
            keep[x * ny + i] += from_x[p, i]
            return carry

        lax.fori_loop(0, ny, add_x, 0)

    def y_copy(k):
        p = lax.rem(y + k, ny)
        return remote(
            keep.at[x * ny + p],
            from_y.at[y],
            plane_sent.at[2, k],
            plane_came.at[2, y],
            (z, x, p, c),
        )

    for k in range(1, ny):
        y_copy(k).start()

    lax.fori_loop(cut[1], steps, step, 0)

    total = keep[x * ny + y]
    for k in range(1, ny):
        p = lax.rem(y + k, ny)
        remote(
            from_y.at[p], from_y.at[p], plane_sent.at[2, k], plane_came.at[2, p], (z, x, p, c)
        ).wait_recv()
        total = total + from_y[p]
    holder = lax.rem(z, group)

    @pl.when(holder != g)
    def _():
        for at in range(per_device):
            scatter(at, at).wait_recv()

    total = total + last[...].reshape(total.shape)
    product[...] = total
    part[...] = lax.dot_general(
        total, total, (((0,), (0,)), ((), ())), precision=HIGHEST, preferred_element_type=jnp.float32
    )

    def rows_of(p):
        return pl.ds(pl.multiple_of(p * strip, strip), strip)

    def exchange(count, peer, stage, mine, source, target_of):
        def copy(k, p, device):
            return remote(
                source(p), target_of(mine), sent.at[stage, k], came.at[stage, mine], device
            )

        def start(k, carry):
            p, device = peer(k)
            copy(k, p, device).start()
            return carry

        def finish(k, carry):
            p, device = peer(k)
            copy(k, p, device).wait_send()
            remote(
                target_of(p), target_of(p), sent.at[stage, k], came.at[stage, p], device
            ).wait_recv()
            return carry

        lax.fori_loop(1, count, start, 0)
        lax.fori_loop(1, count, finish, 0)

    exchange(plane, plane_peer, 0, me, lambda p: part.at[rows_of(p)], lambda p: got.at[p])
    strip_sum = part[rows_of(me)]
    for k in range(1, plane):
        strip_sum = strip_sum + got[lax.rem(me + k, plane)]
    ring[z] = strip_sum
    exchange(nz, ring_peer, 1, z, lambda p: ring.at[z], lambda p: ring.at[p])
    strip_sum = ring[0]
    for k in range(1, nz):
        strip_sum = strip_sum + ring[k]
    whole[rows_of(me)] = strip_sum
    exchange(
        plane, plane_peer, 2, me, lambda p: whole.at[rows_of(me)], lambda p: whole.at[rows_of(p)]
    )
    gram[...] = whole[...]

    for k in range(1, nx):
        x_copy(k).wait_send()
    for k in range(1, ny):
        y_copy(k).wait_send()

    def drain(j, carry):
        up(j).wait_send()

        @pl.when(jnp.logical_not(target))
        def _():
            down(j).wait_send()

        @pl.when(jnp.logical_and(target, j // per_device != g))
        def _():
            scatter(j, lax.rem(j, per_device)).wait_send()

        return carry

    lax.fori_loop(0, chunks, drain, 0)


def device_sums(fwd, bwd):
    sizes = axis_sizes()
    nz, nx, ny, nc = sizes
    group = ny * nc
    plane = nx * group
    _, rows, width = fwd.shape
    strip = width // plane
    most = max(plane, nz)
    chunks = group * rows // CHUNK
    fwd = fwd.reshape(nx * ny, nc, rows, width)
    bwd = bwd.reshape(2, chunks, CHUNK, width)
    vmem = pl.BlockSpec(memory_space=pltpu.VMEM)
    anywhere = pl.BlockSpec(memory_space=pl.ANY)

    def buffer(*shape):
        return pltpu.VMEM(shape, jnp.float32)

    dma = pltpu.SemaphoreType.DMA
    return pl.pallas_call(
        functools.partial(sums_kernel, sizes),
        out_shape=[
            jax.ShapeDtypeStruct((rows, width), jnp.float32),
            jax.ShapeDtypeStruct((width, width), jnp.float32),
        ],
        in_specs=[anywhere, anywhere],
        out_specs=[vmem, vmem],
        scratch_shapes=[
            buffer(2, chunks, CHUNK, width),
            buffer(nx * ny, rows, width),
            buffer(nx * ny, rows, width),
            buffer(nx, ny, rows, width),
            buffer(ny, rows, width),
            buffer(chunks, CHUNK, width),
            buffer(chunks, CHUNK, width),
            buffer(rows // CHUNK, CHUNK, width),
            buffer(width, width),
            buffer(plane, strip, width),
            buffer(nz, strip, width),
            buffer(width, width),
            dma((2,)),
            dma((2, chunks)),
            dma((2, chunks)),
            dma((chunks,)),
            dma((rows // CHUNK,)),
            dma((3, max(nx, ny))),
            dma((3, max(nx, ny))),
            dma((3, most)),
            dma((3, most)),
        ],
        compiler_params=pltpu.CompilerParams(
            collective_id=0, has_side_effects=True, vmem_limit_bytes=VMEM_LIMIT
        ),
        name="device_sums",
    )(fwd, bwd)


def dot_high(a, b, dims):
    return lax.dot_general(
        a, b, (dims, ((), ())), precision=HIGHEST, preferred_element_type=jnp.float32
    )


def inverse_factor(a):
    n = a.shape[0]
    sub = 8
    lanes = lax.broadcasted_iota(jnp.int32, (sub, n), 1)
    subs = lax.broadcasted_iota(jnp.int32, (sub, n), 0)
    left = [a[i * sub : (i + 1) * sub] for i in range(n // sub)]
    right = [(lanes == subs + i * sub).astype(jnp.float32) for i in range(n // sub)]
    for j in range(n):
        t0, s = divmod(j, sub)
        row = left[t0][s : s + 1]
        inv = 1.0 / row[:, j : j + 1]
        wrow = right[t0][s : s + 1]
        scaled = row * inv
        wscaled = wrow * inv
        for t in range(t0, n // sub):
            col = left[t][:, j : j + 1]
            if t == t0:
                col = jnp.where(subs[:, :1] > s, col, 0.0)
            left[t] = left[t] - col * scaled
            right[t] = right[t] - col * wscaled
    out = []
    for t in range(n // sub):
        d = jnp.sum(jnp.where(lanes == subs + t * sub, left[t], 0.0), axis=1, keepdims=True)
        out.append(right[t] * lax.rsqrt(d))
    return jnp.concatenate(out, axis=0)


def basis_kernel(scale, gram, product, basis):
    n = gram.shape[0]
    h = n // 2
    g11 = gram[:h, :h] * scale
    g21 = gram[h:, :h] * scale
    g22 = gram[h:, h:] * scale
    w11 = inverse_factor(g11)
    l21 = dot_high(g21, w11, ((1,), (1,)))
    w22 = inverse_factor(g22 - dot_high(l21, l21, ((1,), (1,))))
    w21 = -dot_high(w22, dot_high(l21, w11, ((1,), (0,))), ((1,), (0,)))
    first = product[:, :h]
    basis[:, :h] = dot_high(first, w11, ((1,), (1,)))
    basis[:, h:] = dot_high(first, w21, ((1,), (1,))) + dot_high(
        product[:, h:], w22, ((1,), (1,))
    )


def new_basis(gram, product, nodes):
    vmem = pl.BlockSpec(memory_space=pltpu.VMEM)
    return pl.pallas_call(
        functools.partial(basis_kernel, 1.0 / nodes),
        out_shape=jax.ShapeDtypeStruct(product.shape, jnp.float32),
        in_specs=[vmem, vmem],
        out_specs=vmem,
        compiler_params=pltpu.CompilerParams(vmem_limit_bytes=VMEM_LIMIT),
        name="new_basis",
    )(gram, product)


def shards(panel, lists, tiles):
    nz, nx, ny, nc = axis_sizes()
    group = ny * nc
    plane = nx * group
    tile = tiles.shape[1]
    width = panel.shape[1]
    blocks = panel.shape[0] // tile
    nodes = panel.shape[0] * nz * plane
    his = nz // group
    sort = (2, 1, 0)
    send = tiles.reshape(his, group, nx, tile, tile).transpose(2, 1, 0, 3, 4)
    here = lax.all_to_all(
        send.reshape(plane, his, tile, tile), PLANE, split_axis=0, concat_axis=0, tiled=True
    )
    send = lists.reshape(3, his, group, nx).transpose(3, 2, 1, 0)
    meta = lax.all_to_all(
        send.reshape(plane, his, 3), PLANE, split_axis=0, concat_axis=0, tiled=True
    )
    meta = meta.reshape(plane * his, 3).T
    own = panel.reshape(blocks, tile, width)
    rows = lax.all_gather(own, PLANE, axis=0)
    column = lax.all_gather(own, "z", axis=0).reshape(his, group, blocks, tile, width)
    cols = lax.all_to_all(
        column.transpose(1, 0, 2, 3, 4), GROUP, split_axis=0, concat_axis=0, tiled=True
    )
    fwd, bwd = tile_products(meta, here, cols, rows)
    product, gram = device_sums(
        fwd.reshape(plane, blocks * tile, width), bwd.reshape(his, group * blocks * tile, width)
    )
    return new_basis(gram, product, nodes)


def solution(mesh):
    sizes = mesh.devices.shape
    nx, ny, nc = grid_of(sizes)
    fine = Mesh(mesh.devices.reshape(sizes[0] // nx, nx, ny, nc), AXES)
    return jax.shard_map(
        shards,
        mesh=fine,
        in_specs=(P(AXES, None), P(None, AXES), P(AXES, None, None)),
        out_specs=P(AXES, None),
        check_vma=False,
    )


def grid_of(sizes):
    return (4, 4, 2) if sizes == (64, 8) else (2, 1, 2)
```

```python
import functools

import jax
import jax.numpy as jnp
from jax import lax
from jax.experimental import pallas as pl
from jax.experimental.pallas import tpu as pltpu
from jax.sharding import Mesh, PartitionSpec as P

HIGHEST = lax.Precision.HIGHEST
MESH = pl.DeviceIdType.MESH
VMEM_LIMIT = 56 * 1024 * 1024
AXES = ("z", "x", "y", "core")


def axis_sizes():
    return tuple(lax.axis_size(a) for a in AXES)


def split2(t):
    high = t.astype(jnp.bfloat16)
    low = (t - high.astype(jnp.float32)).astype(jnp.bfloat16)
    return high, low


PASS = 2


def bring_kernel(
    sizes,
    panel,
    lists,
    tiles,
    here,
    meta,
    cols,
    rows,
    local_sem,
    tile_sent,
    tile_came,
    list_sent,
    list_came,
    gather_sent,
    gather_came,
    chain_sent,
    chain_came,
    first_sent,
    first_came,
    second_sent,
    second_came,
    core_sent,
    core_came,
):
    nz, nx, ny, nc = sizes
    group = ny * nc
    plane = nx * group
    half = nz // 2
    z, x, y, c = (lax.axis_index(a) for a in AXES)
    g = y * nc + c
    me = x * group + g
    blocks = panel.shape[0]
    chunks = cols.shape[1]

    def member(p):
        return (z, x, p // nc, lax.rem(p, nc))

    def plane_peer(k):
        p = lax.rem(me + k, plane)
        return p, (z, p // group, lax.rem(p, group) // nc, lax.rem(p, nc))

    def remote(source, target, send_sem, recv_sem, device):
        return pltpu.make_async_remote_copy(
            src_ref=source,
            dst_ref=target,
            send_sem=send_sem,
            recv_sem=recv_sem,
            device_id=device,
            device_id_type=MESH,
        )

    above = (lax.rem(z + 1, nz), x, y, c)
    below = (lax.rem(z + nz - 1, nz), x, y, c)
    other = (z, x, y, nc - 1 - c)

    barrier = pltpu.get_barrier_semaphore()

    def greet(k, carry):
        pl.semaphore_signal(barrier, inc=1, device_id=plane_peer(k)[1], device_id_type=MESH)
        return carry

    lax.fori_loop(1, plane, greet, 0)
    for device in (above, below):
        pl.semaphore_signal(barrier, inc=1, device_id=device, device_id_type=MESH)

    holder = lax.rem(z, group)
    his = z // group
    place = g * nx + x
    local = [
        pltpu.make_async_copy(panel, rows.at[x, y, c], local_sem.at[0]),
        pltpu.make_async_copy(tiles.at[:, place], here.at[me], local_sem.at[1]),
        pltpu.make_async_copy(lists, meta.at[me], local_sem.at[2]),
    ]
    to_cols = pltpu.make_async_copy(
        panel, cols.at[his, pl.ds(g * blocks, blocks)], local_sem.at[3]
    )
    for copy in local:
        copy.start()

    @pl.when(holder == g)
    def _():
        to_cols.start()

    pl.semaphore_wait(barrier, plane - 1 + 2)

    def gather(p):
        return remote(
            panel,
            cols.at[his, pl.ds(p * blocks, blocks)],
            gather_sent.at[0],
            gather_came.at[p],
            member(holder),
        )

    @pl.when(holder != g)
    def _():
        gather(g).start()

    def first_x(k, p, at):
        return remote(
            panel.at[0], rows.at[at, y, c, 0], first_sent.at[0, k], first_came.at[0, at], (z, p, y, c)
        )

    def first_y(k, p, at):
        return remote(
            panel.at[1], rows.at[x, at, c, 1], first_sent.at[1, k], first_came.at[1, at], (z, x, p, c)
        )

    for k in range(1, nx):
        first_x(k, lax.rem(x + k, nx), x).start()
    for k in range(1, ny):
        first_y(k, lax.rem(y + k, ny), y).start()

    def tile_copy(k, p, device, at):
        to = lax.rem(p, group) * nx + p // group
        return remote(tiles.at[:, to], here.at[at], tile_sent.at[k], tile_came.at[at], device)

    def list_copy(k, device, at):
        return remote(lists, meta.at[at], list_sent.at[k], list_came.at[at], device)

    def start_tiles(k, carry):
        p, device = plane_peer(k)
        list_copy(k, device, me).start()
        tile_copy(k, p, device, me).start()
        return carry

    lax.fori_loop(1, plane, start_tiles, 0)

    d0 = lax.rem(g - z + nz, nz)
    lower = jnp.logical_and(d0 >= 1, d0 <= half)
    hu = jnp.where(lower, 0, 1)
    hd = 1 - hu
    du = jnp.where(lower, d0, lax.rem(d0 + half, nz))
    dd = half - du
    origin = du == half

    def down(h, j):
        return remote(
            cols.at[h, j], cols.at[h, j], chain_sent.at[0, j], chain_came.at[0, j], below
        )

    def up(h, j):
        return remote(
            cols.at[h, j], cols.at[h, j], chain_sent.at[1, j], chain_came.at[1, j], above
        )

    @pl.when(origin)
    def _():
        to_cols.wait()
        for p in range(group):

            @pl.when(p != g)
            def _(p=p):
                gather(p).wait_recv()

        def begin(j, carry):
            down(hd, j).start()
            up(hd, j).start()
            return carry

        lax.fori_loop(0, chunks, begin, 0)

    def step(i, carry):
        j = i - PASS * (du - 1)

        @pl.when(jnp.logical_and(j >= 0, j < chunks))
        def _():
            down(hu, j).wait_recv()

            @pl.when(du < half)
            def _():
                down(hu, j).start()

        ju = i - PASS * (dd - 1)

        @pl.when(jnp.logical_and(jnp.logical_not(origin), jnp.logical_and(ju >= 0, ju < chunks)))
        def _():
            up(hd, ju).wait_recv()

            @pl.when(dd < half - 1)
            def _():
                up(hd, ju).start()

        return carry

    steps = chunks + PASS * (half - 1)
    cut = (steps // 3, (2 * steps) // 3)
    lax.fori_loop(0, cut[0], step, 0)

    def second_y(k, p, at):
        part = rows.at[:, at, c, 0]
        return remote(part, part, second_sent.at[0, k], second_came.at[0, at], (z, x, p, c))

    def second_x(k, p, at):
        part = rows.at[at, :, c, 1]
        return remote(part, part, second_sent.at[1, k], second_came.at[1, at], (z, p, y, c))

    for copy in local:
        copy.wait()
    for k in range(1, nx):
        p = lax.rem(x + k, nx)
        first_x(k, p, p).wait_recv()
    for k in range(1, ny):
        second_y(k, lax.rem(y + k, ny), y).start()
    for k in range(1, ny):
        p = lax.rem(y + k, ny)
        first_y(k, p, p).wait_recv()
    for k in range(1, nx):
        second_x(k, lax.rem(x + k, nx), x).start()

    lax.fori_loop(cut[0], cut[1], step, 0)

    def core_y(p, of):
        part = rows.at[:, p, of, 0]
        return remote(part, part, core_sent.at[0, p], core_came.at[0, p], other)

    def core_x(p, of):
        part = rows.at[p, :, of, 1]
        return remote(part, part, core_sent.at[1, p], core_came.at[1, p], other)

    core_y(y, c).start()
    core_x(x, c).start()
    for k in range(1, ny):
        p = lax.rem(y + k, ny)
        second_y(k, p, p).wait_recv()
        core_y(p, c).start()
    for k in range(1, nx):
        p = lax.rem(x + k, nx)
        second_x(k, p, p).wait_recv()
        core_x(p, c).start()

    lax.fori_loop(cut[1], steps, step, 0)

    def finish(k, carry):
        p, device = plane_peer(k)
        tile_copy(k, p, device, p).wait_recv()
        list_copy(k, device, p).wait_recv()
        tile_copy(k, p, device, me).wait_send()
        list_copy(k, device, me).wait_send()
        return carry

    lax.fori_loop(1, plane, finish, 0)
    for p in range(ny):
        core_y(p, nc - 1 - c).wait_recv()
        core_y(p, c).wait_send()
    for p in range(nx):
        core_x(p, nc - 1 - c).wait_recv()
        core_x(p, c).wait_send()
    for k in range(1, nx):
        p = lax.rem(x + k, nx)
        first_x(k, p, x).wait_send()
        second_x(k, p, x).wait_send()
    for k in range(1, ny):
        p = lax.rem(y + k, ny)
        first_y(k, p, y).wait_send()
        second_y(k, p, y).wait_send()

    @pl.when(holder != g)
    def _():
        gather(g).wait_send()

    def drain(j, carry):
        @pl.when(origin)
        def _():
            down(hd, j).wait_send()
            up(hd, j).wait_send()

        @pl.when(du < half)
        def _():
            down(hu, j).wait_send()

        @pl.when(jnp.logical_and(jnp.logical_not(origin), dd < half - 1))
        def _():
            up(hd, j).wait_send()

        return carry

    lax.fori_loop(0, chunks, drain, 0)


def bring(panel, lists, tiles):
    sizes = axis_sizes()
    nz, nx, ny, nc = sizes
    group = ny * nc
    plane = nx * group
    blocks, tile, width = panel.shape
    his = nz // group
    span = group * blocks
    anywhere = pl.BlockSpec(memory_space=pl.ANY)
    dma = pltpu.SemaphoreType.DMA
    most = max(nx, ny)
    return pl.pallas_call(
        functools.partial(bring_kernel, sizes),
        out_shape=[
            jax.ShapeDtypeStruct((plane, his, tile, tile), jnp.float32),
            jax.ShapeDtypeStruct((plane,) + lists.shape, jnp.int32),
            jax.ShapeDtypeStruct((his, span, tile, width), jnp.bfloat16),
            jax.ShapeDtypeStruct((nx, ny, nc, blocks, tile, width), jnp.bfloat16),
        ],
        in_specs=[anywhere] * 3,
        out_specs=[anywhere] * 4,
        scratch_shapes=[
            dma((4,)),
            dma((plane,)),
            dma((plane,)),
            dma((plane,)),
            dma((plane,)),
            dma((1,)),
            dma((group,)),
            dma((2, span)),
            dma((2, span)),
            dma((2, most)),
            dma((2, most)),
            dma((2, most)),
            dma((2, most)),
            dma((2, most)),
            dma((2, most)),
        ],
        compiler_params=pltpu.CompilerParams(
            collective_id=1, has_side_effects=True, vmem_limit_bytes=VMEM_LIMIT
        ),
        name="bring",
    )(panel, lists, tiles)


def tiles_kernel(his, blocks, span, step, meta, tiles, cols, rows, fwd, bwd):
    at = pl.program_id(0)

    @pl.when(at == 0)
    def _():
        bwd[...] = jnp.zeros_like(bwd)

    for u in range(step):
        src = at * step + u
        values, panels, picks = [], [], []
        for hi in range(his):
            slot = src * his + hi
            row, col, live = meta[0, slot], meta[1, slot], meta[2, slot]
            t = tiles[u, hi] * live.astype(jnp.float32)
            values.append(t)
            picks.append(row)
            panels.append(cols[hi, col])
            flipped = jnp.concatenate(split2(t.T), axis=1)
            own = rows[u, row]
            got = jnp.dot(
                flipped, jnp.concatenate([own, own], axis=0), preferred_element_type=jnp.float32
            )
            bwd[hi, col] += got
        left = jnp.concatenate(
            [
                jnp.concatenate(
                    [t * (pick == b).astype(jnp.float32) for t, pick in zip(values, picks)], axis=1
                )
                for b in range(blocks)
            ],
            axis=0,
        )
        right = jnp.concatenate(panels, axis=0)
        high, low = split2(left)
        out = jnp.dot(high, right, preferred_element_type=jnp.float32) + jnp.dot(
            low, right, preferred_element_type=jnp.float32
        )
        fwd[u] = out.reshape(fwd.shape[1:])


def tile_products(meta, tiles, cols, rows):
    plane, his, tile, _ = tiles.shape
    blocks, width = rows.shape[1], rows.shape[3]
    span = cols.shape[1]
    step = 4
    return pl.pallas_call(
        functools.partial(tiles_kernel, his, blocks, span, step),
        grid_spec=pltpu.PrefetchScalarGridSpec(
            num_scalar_prefetch=1,
            grid=(plane // step,),
            in_specs=[
                pl.BlockSpec((step, his, tile, tile), lambda i, m: (i, 0, 0, 0)),
                pl.BlockSpec(cols.shape, lambda i, m: (0, 0, 0, 0)),
                pl.BlockSpec((step, blocks, tile, width), lambda i, m: (i, 0, 0, 0)),
            ],
            out_specs=[
                pl.BlockSpec((step, blocks, tile, width), lambda i, m: (i, 0, 0, 0)),
                pl.BlockSpec((his, span, tile, width), lambda i, m: (0, 0, 0, 0)),
            ],
        ),
        out_shape=[
            jax.ShapeDtypeStruct((plane, blocks, tile, width), jnp.float32),
            jax.ShapeDtypeStruct((his, span, tile, width), jnp.float32),
        ],
        compiler_params=pltpu.CompilerParams(vmem_limit_bytes=VMEM_LIMIT),
        name="tile_products",
    )(meta, tiles, cols, rows)


CHUNK = 64
SKEW = 2


def sums_kernel(
    sizes,
    fwd,
    bwd,
    product,
    gram,
    held,
    keep,
    from_core,
    from_x,
    from_y,
    from_below,
    from_above,
    last,
    part,
    got,
    ring,
    whole,
    local_sem,
    chain_sent,
    chain_came,
    last_sent,
    last_came,
    plane_sent,
    plane_came,
    sent,
    came,
):
    nz, nx, ny, nc = sizes
    group = ny * nc
    plane = nx * group
    half = nz // 2
    z, x, y, c = (lax.axis_index(a) for a in AXES)
    g = y * nc + c
    me = x * group + g
    strip = part.shape[0] // plane
    chunks = held.shape[1]
    per_device = last.shape[0]

    def member(p):
        return (z, x, p // nc, lax.rem(p, nc))

    def plane_peer(k):
        p = lax.rem(me + k, plane)
        return p, (z, p // group, lax.rem(p, group) // nc, lax.rem(p, nc))

    def ring_peer(k):
        q = lax.rem(z + k, nz)
        return q, (q, x, y, c)

    def remote(source, target, send_sem, recv_sem, device):
        return pltpu.make_async_remote_copy(
            src_ref=source,
            dst_ref=target,
            send_sem=send_sem,
            recv_sem=recv_sem,
            device_id=device,
            device_id_type=MESH,
        )

    barrier = pltpu.get_barrier_semaphore()

    def greet(peer):
        def body(k, carry):
            pl.semaphore_signal(barrier, inc=1, device_id=peer(k)[1], device_id_type=MESH)
            return carry

        return body

    lax.fori_loop(1, plane, greet(plane_peer), 0)
    lax.fori_loop(1, nz, greet(ring_peer), 0)
    load_held = pltpu.make_async_copy(bwd, held, local_sem.at[0])
    load_keep = pltpu.make_async_copy(fwd.at[:, c], keep, local_sem.at[1])
    load_held.start()
    load_keep.start()
    pl.semaphore_wait(barrier, plane - 1 + nz - 1)

    other = (z, x, y, nc - 1 - c)
    core_copy = remote(
        fwd.at[:, nc - 1 - c], from_core, plane_sent.at[0, 0], plane_came.at[0, 0], other
    )
    core_copy.start()

    d0 = lax.rem(g - z + nz, nz)
    lower = jnp.logical_and(d0 >= 1, d0 <= half)
    hu = jnp.where(lower, 0, 1)
    hd = 1 - hu
    du = jnp.where(lower, d0, lax.rem(d0 + half, nz))
    pu = half - du
    pd = du - 1
    target = du == half
    above = (lax.rem(z + 1, nz), x, y, c)
    below = (lax.rem(z + nz - 1, nz), x, y, c)

    def up(j):
        return remote(
            held.at[hu, j], from_below.at[j], chain_sent.at[0, j], chain_came.at[0, j], above
        )

    def down(j):
        return remote(
            held.at[hd, j], from_above.at[j], chain_sent.at[1, j], chain_came.at[1, j], below
        )

    def scatter(j, at):
        return remote(
            held.at[hd, j], last.at[at], last_sent.at[j], last_came.at[at], member(j // per_device)
        )

    load_held.wait()

    def step(i, carry):
        j = i - SKEW * pu

        @pl.when(jnp.logical_and(j >= 0, j < chunks))
        def _():
            @pl.when(pu > 0)
            def _():
                up(j).wait_recv()
                held[hu, j] += from_below[j]

            up(j).start()

        jd = i - SKEW * pd

        @pl.when(jnp.logical_and(jnp.logical_not(target), jnp.logical_and(jd >= 0, jd < chunks)))
        def _():
            @pl.when(pd > 0)
            def _():
                down(jd).wait_recv()
                held[hd, jd] += from_above[jd]

            down(jd).start()

        jt = i - SKEW * half

        @pl.when(jnp.logical_and(target, jnp.logical_and(jt >= 0, jt < chunks)))
        def _():
            up(jt).wait_recv()
            down(jt).wait_recv()
            held[hd, jt] += from_below[jt] + from_above[jt]
            at = lax.rem(jt, per_device)

            @pl.when(jt // per_device == g)
            def _():
                last[at] = held[hd, jt]

            @pl.when(jt // per_device != g)
            def _():
                scatter(jt, at).start()

        return carry

    steps = chunks + SKEW * half
    cut = (steps // 5, (3 * steps) // 4)
    lax.fori_loop(0, cut[0], step, 0)

    load_keep.wait()
    core_copy.wait()

    def x_copy(k):
        p = lax.rem(x + k, nx)
        return remote(
            keep.at[pl.ds(p * ny, ny)],
            from_x.at[x],
            plane_sent.at[1, k],
            plane_came.at[1, x],
            (z, p, y, c),
        )

    def x_source(k):
        p = lax.rem(x + k, nx)
        return p, remote(
            from_x.at[p], from_x.at[p], plane_sent.at[1, k], plane_came.at[1, p], (z, p, y, c)
        )

    for k in range(1, nx + 1):
        p = lax.rem(x + k, nx)

        def add_core(i, carry, p=p):
            keep[p * ny + i] += from_core[p * ny + i]
            return carry

        lax.fori_loop(0, ny, add_core, 0)
        if k < nx:
            x_copy(k).start()

    lax.fori_loop(cut[0], cut[1], step, 0)

    for k in range(1, nx):
        p, copy = x_source(k)
        copy.wait_recv()

        def add_x(i, carry, p=p):
            keep[x * ny + i] += from_x[p, i]
            return carry

        lax.fori_loop(0, ny, add_x, 0)

    def y_copy(k):
        p = lax.rem(y + k, ny)
        return remote(
            keep.at[x * ny + p],
            from_y.at[y],
            plane_sent.at[2, k],
            plane_came.at[2, y],
            (z, x, p, c),
        )

    for k in range(1, ny):
        y_copy(k).start()

    lax.fori_loop(cut[1], steps, step, 0)

    total = keep[x * ny + y]
    for k in range(1, ny):
        p = lax.rem(y + k, ny)
        remote(
            from_y.at[p], from_y.at[p], plane_sent.at[2, k], plane_came.at[2, p], (z, x, p, c)
        ).wait_recv()
        total = total + from_y[p]
    holder = lax.rem(z, group)

    @pl.when(holder != g)
    def _():
        for at in range(per_device):
            scatter(at, at).wait_recv()

    total = total + last[...].reshape(total.shape)
    product[...] = total
    part[...] = lax.dot_general(
        total, total, (((0,), (0,)), ((), ())), precision=HIGHEST, preferred_element_type=jnp.float32
    )

    def rows_of(p):
        return pl.ds(pl.multiple_of(p * strip, strip), strip)

    def exchange(count, peer, stage, mine, source, target_of):
        def copy(k, p, device):
            return remote(
                source(p), target_of(mine), sent.at[stage, k], came.at[stage, mine], device
            )

        def start(k, carry):
            p, device = peer(k)
            copy(k, p, device).start()
            return carry

        def finish(k, carry):
            p, device = peer(k)
            copy(k, p, device).wait_send()
            remote(
                target_of(p), target_of(p), sent.at[stage, k], came.at[stage, p], device
            ).wait_recv()
            return carry

        lax.fori_loop(1, count, start, 0)
        lax.fori_loop(1, count, finish, 0)

    exchange(plane, plane_peer, 0, me, lambda p: part.at[rows_of(p)], lambda p: got.at[p])
    strip_sum = part[rows_of(me)]
    for k in range(1, plane):
        strip_sum = strip_sum + got[lax.rem(me + k, plane)]
    ring[z] = strip_sum
    exchange(nz, ring_peer, 1, z, lambda p: ring.at[z], lambda p: ring.at[p])
    strip_sum = ring[0]
    for k in range(1, nz):
        strip_sum = strip_sum + ring[k]
    whole[rows_of(me)] = strip_sum
    exchange(
        plane, plane_peer, 2, me, lambda p: whole.at[rows_of(me)], lambda p: whole.at[rows_of(p)]
    )
    gram[...] = whole[...]

    for k in range(1, nx):
        x_copy(k).wait_send()
    for k in range(1, ny):
        y_copy(k).wait_send()

    def drain(j, carry):
        up(j).wait_send()

        @pl.when(jnp.logical_not(target))
        def _():
            down(j).wait_send()

        @pl.when(jnp.logical_and(target, j // per_device != g))
        def _():
            scatter(j, lax.rem(j, per_device)).wait_send()

        return carry

    lax.fori_loop(0, chunks, drain, 0)


def device_sums(fwd, bwd):
    sizes = axis_sizes()
    nz, nx, ny, nc = sizes
    group = ny * nc
    plane = nx * group
    _, rows, width = fwd.shape
    strip = width // plane
    most = max(plane, nz)
    chunks = group * rows // CHUNK
    fwd = fwd.reshape(nx * ny, nc, rows, width)
    bwd = bwd.reshape(2, chunks, CHUNK, width)
    vmem = pl.BlockSpec(memory_space=pltpu.VMEM)
    anywhere = pl.BlockSpec(memory_space=pl.ANY)

    def buffer(*shape):
        return pltpu.VMEM(shape, jnp.float32)

    dma = pltpu.SemaphoreType.DMA
    return pl.pallas_call(
        functools.partial(sums_kernel, sizes),
        out_shape=[
            jax.ShapeDtypeStruct((rows, width), jnp.float32),
            jax.ShapeDtypeStruct((width, width), jnp.float32),
        ],
        in_specs=[anywhere, anywhere],
        out_specs=[vmem, vmem],
        scratch_shapes=[
            buffer(2, chunks, CHUNK, width),
            buffer(nx * ny, rows, width),
            buffer(nx * ny, rows, width),
            buffer(nx, ny, rows, width),
            buffer(ny, rows, width),
            buffer(chunks, CHUNK, width),
            buffer(chunks, CHUNK, width),
            buffer(rows // CHUNK, CHUNK, width),
            buffer(width, width),
            buffer(plane, strip, width),
            buffer(nz, strip, width),
            buffer(width, width),
            dma((2,)),
            dma((2, chunks)),
            dma((2, chunks)),
            dma((chunks,)),
            dma((rows // CHUNK,)),
            dma((3, max(nx, ny))),
            dma((3, max(nx, ny))),
            dma((3, most)),
            dma((3, most)),
        ],
        compiler_params=pltpu.CompilerParams(
            collective_id=0, has_side_effects=True, vmem_limit_bytes=VMEM_LIMIT
        ),
        name="device_sums",
    )(fwd, bwd)


def dot_high(a, b, dims):
    return lax.dot_general(
        a, b, (dims, ((), ())), precision=HIGHEST, preferred_element_type=jnp.float32
    )


def inverse_factor(a):
    n = a.shape[0]
    sub = 8
    lanes = lax.broadcasted_iota(jnp.int32, (sub, n), 1)
    subs = lax.broadcasted_iota(jnp.int32, (sub, n), 0)
    left = [a[i * sub : (i + 1) * sub] for i in range(n // sub)]
    right = [(lanes == subs + i * sub).astype(jnp.float32) for i in range(n // sub)]
    for j in range(n):
        t0, s = divmod(j, sub)
        row = left[t0][s : s + 1]
        inv = 1.0 / row[:, j : j + 1]
        wrow = right[t0][s : s + 1]
        scaled = row * inv
        wscaled = wrow * inv
        for t in range(t0, n // sub):
            col = left[t][:, j : j + 1]
            if t == t0:
                col = jnp.where(subs[:, :1] > s, col, 0.0)
            left[t] = left[t] - col * scaled
            right[t] = right[t] - col * wscaled
    out = []
    for t in range(n // sub):
        d = jnp.sum(jnp.where(lanes == subs + t * sub, left[t], 0.0), axis=1, keepdims=True)
        out.append(right[t] * lax.rsqrt(d))
    return jnp.concatenate(out, axis=0)


def basis_kernel(scale, gram, product, basis):
    n = gram.shape[0]
    h = n // 2
    g11 = gram[:h, :h] * scale
    g21 = gram[h:, :h] * scale
    g22 = gram[h:, h:] * scale
    w11 = inverse_factor(g11)
    l21 = dot_high(g21, w11, ((1,), (1,)))
    w22 = inverse_factor(g22 - dot_high(l21, l21, ((1,), (1,))))
    w21 = -dot_high(w22, dot_high(l21, w11, ((1,), (0,))), ((1,), (0,)))
    first = product[:, :h]
    basis[:, :h] = dot_high(first, w11, ((1,), (1,)))
    basis[:, h:] = dot_high(first, w21, ((1,), (1,))) + dot_high(
        product[:, h:], w22, ((1,), (1,))
    )


def new_basis(gram, product, nodes):
    vmem = pl.BlockSpec(memory_space=pltpu.VMEM)
    return pl.pallas_call(
        functools.partial(basis_kernel, 1.0 / nodes),
        out_shape=jax.ShapeDtypeStruct(product.shape, jnp.float32),
        in_specs=[vmem, vmem],
        out_specs=vmem,
        compiler_params=pltpu.CompilerParams(vmem_limit_bytes=VMEM_LIMIT),
        name="new_basis",
    )(gram, product)


def shards(panel, lists, tiles):
    nz, nx, ny, nc = axis_sizes()
    group = ny * nc
    plane = nx * group
    tile = tiles.shape[1]
    width = panel.shape[1]
    blocks = panel.shape[0] // tile
    nodes = panel.shape[0] * nz * plane
    his = nz // group
    own = panel.reshape(blocks, tile, width)
    here, meta, cols, rows = bring(
        own,
        jnp.pad(lists, ((0, 8 - 3), (0, 128 - lists.shape[1] % 128))),
        tiles.reshape(his, group * nx, tile, tile),
    )
    place = (lax.axis_index("y") * nc + lax.axis_index("core")) * nx + lax.axis_index("x")
    meta = meta[:, :3, : lists.shape[1]].reshape(plane, 3, his, group * nx)
    meta = lax.dynamic_index_in_dim(meta, place, 3, keepdims=False)
    meta = meta.transpose(1, 0, 2).reshape(3, plane * his)
    rows = rows.reshape(plane, blocks, tile, width)
    fwd, bwd = tile_products(meta, here, cols, rows)
    product, gram = device_sums(
        fwd.reshape(plane, blocks * tile, width), bwd.reshape(his, group * blocks * tile, width)
    )
    return new_basis(gram, product, nodes)


def solution(mesh):
    sizes = mesh.devices.shape
    nx, ny, nc = grid_of(sizes)
    fine = Mesh(mesh.devices.reshape(sizes[0] // nx, nx, ny, nc), AXES)
    return jax.shard_map(
        shards,
        mesh=fine,
        in_specs=(P(AXES, None), P(None, AXES), P(AXES, None, None)),
        out_specs=P(AXES, None),
        check_vma=False,
    )


def grid_of(sizes):
    return (4, 4, 2) if sizes == (64, 8) else (2, 1, 2)
```

```python
import functools

import jax
import jax.numpy as jnp
from jax import lax
from jax.experimental import pallas as pl
from jax.experimental.pallas import tpu as pltpu
from jax.sharding import Mesh, PartitionSpec as P

HIGHEST = lax.Precision.HIGHEST
MESH = pl.DeviceIdType.MESH
VMEM_LIMIT = 56 * 1024 * 1024
AXES = ("z", "x", "y", "core")


def axis_sizes():
    return tuple(lax.axis_size(a) for a in AXES)


def split2(t):
    high = t.astype(jnp.bfloat16)
    low = (t - high.astype(jnp.float32)).astype(jnp.bfloat16)
    return high, low


PASS = 3


def bring_kernel(
    sizes,
    panel,
    lists,
    tiles,
    here,
    meta,
    cols,
    rows,
    local_sem,
    tile_sent,
    tile_came,
    list_sent,
    list_came,
    gather_sent,
    gather_came,
    chain_sent,
    chain_came,
    first_sent,
    first_came,
    second_sent,
    second_came,
    core_sent,
    core_came,
):
    nz, nx, ny, nc = sizes
    group = ny * nc
    plane = nx * group
    half = nz // 2
    z, x, y, c = (lax.axis_index(a) for a in AXES)
    g = y * nc + c
    me = x * group + g
    blocks = panel.shape[0]
    chunks = cols.shape[1]

    def member(p):
        return (z, x, p // nc, lax.rem(p, nc))

    def plane_peer(k):
        across = lax.rem(k, nx)
        px = lax.rem(x + across, nx)
        py = lax.rem(y + lax.rem(k // nx, ny) + across, ny)
        pc = lax.rem(c + k // (nx * ny), nc)
        return px * group + py * nc + pc, (z, px, py, pc)

    def remote(source, target, send_sem, recv_sem, device):
        return pltpu.make_async_remote_copy(
            src_ref=source,
            dst_ref=target,
            send_sem=send_sem,
            recv_sem=recv_sem,
            device_id=device,
            device_id_type=MESH,
        )

    above = (lax.rem(z + 1, nz), x, y, c)
    below = (lax.rem(z + nz - 1, nz), x, y, c)
    other = (z, x, y, nc - 1 - c)

    barrier = pltpu.get_barrier_semaphore()

    def greet(k, carry):
        pl.semaphore_signal(barrier, inc=1, device_id=plane_peer(k)[1], device_id_type=MESH)
        return carry

    lax.fori_loop(1, plane, greet, 0)
    for device in (above, below):
        pl.semaphore_signal(barrier, inc=1, device_id=device, device_id_type=MESH)

    holder = lax.rem(z, group)
    his = z // group
    place = g * nx + x
    local = [
        pltpu.make_async_copy(panel, rows.at[x, y, c], local_sem.at[0]),
        pltpu.make_async_copy(tiles.at[:, place], here.at[me], local_sem.at[1]),
        pltpu.make_async_copy(lists, meta.at[me], local_sem.at[2]),
    ]
    to_cols = pltpu.make_async_copy(
        panel, cols.at[his, pl.ds(g * blocks, blocks)], local_sem.at[3]
    )
    for copy in local:
        copy.start()

    @pl.when(holder == g)
    def _():
        to_cols.start()

    pl.semaphore_wait(barrier, plane - 1 + 2)

    def gather(p):
        return remote(
            panel,
            cols.at[his, pl.ds(p * blocks, blocks)],
            gather_sent.at[0],
            gather_came.at[p],
            member(holder),
        )

    @pl.when(holder != g)
    def _():
        gather(g).start()

    def first_x(k, p, at):
        return remote(
            panel.at[0], rows.at[at, y, c, 0], first_sent.at[0, k], first_came.at[0, at], (z, p, y, c)
        )

    def first_y(k, p, at):
        return remote(
            panel.at[1], rows.at[x, at, c, 1], first_sent.at[1, k], first_came.at[1, at], (z, x, p, c)
        )

    for k in range(1, nx):
        first_x(k, lax.rem(x + k, nx), x).start()
    for k in range(1, ny):
        first_y(k, lax.rem(y + k, ny), y).start()

    def tile_copy(k, p, device, at):
        to = lax.rem(p, group) * nx + p // group
        return remote(tiles.at[:, to], here.at[at], tile_sent.at[k], tile_came.at[at], device)

    def list_copy(k, device, at):
        return remote(lists, meta.at[at], list_sent.at[k], list_came.at[at], device)

    def start_tiles(k, carry):
        p, device = plane_peer(k)
        list_copy(k, device, me).start()
        tile_copy(k, p, device, me).start()
        return carry

    lax.fori_loop(1, plane, start_tiles, 0)

    d0 = lax.rem(g - z + nz, nz)
    lower = jnp.logical_and(d0 >= 1, d0 <= half)
    hu = jnp.where(lower, 0, 1)
    hd = 1 - hu
    du = jnp.where(lower, d0, lax.rem(d0 + half, nz))
    dd = half - du
    origin = du == half

    def down(h, j):
        return remote(
            cols.at[h, j], cols.at[h, j], chain_sent.at[0, j], chain_came.at[0, j], below
        )

    def up(h, j):
        return remote(
            cols.at[h, j], cols.at[h, j], chain_sent.at[1, j], chain_came.at[1, j], above
        )

    def in_turn(j):
        return lax.rem(g + j // blocks, group) * blocks + lax.rem(j, blocks)

    @pl.when(origin)
    def _():
        to_cols.wait()
        for m in range(group):
            if m > 0:
                gather(lax.rem(g + m, group)).wait_recv()
            for b in range(blocks):
                down(hd, in_turn(m * blocks + b)).start()
                up(hd, in_turn(m * blocks + b)).start()

    def step(i, carry):
        j = i - PASS * (du - 1)

        @pl.when(jnp.logical_and(j >= 0, j < chunks))
        def _():
            down(hu, in_turn(j)).wait_recv()

            @pl.when(du < half)
            def _():
                down(hu, in_turn(j)).start()

        ju = i - PASS * (dd - 1)

        @pl.when(jnp.logical_and(jnp.logical_not(origin), jnp.logical_and(ju >= 0, ju < chunks)))
        def _():
            up(hd, in_turn(ju)).wait_recv()

            @pl.when(dd < half - 1)
            def _():
                up(hd, in_turn(ju)).start()

        return carry

    steps = chunks + PASS * (half - 1)
    cut = (steps // 3, (2 * steps) // 3)
    lax.fori_loop(0, cut[0], step, 0)

    def second_y(k, p, at):
        part = rows.at[:, at, c, 0]
        return remote(part, part, second_sent.at[0, k], second_came.at[0, at], (z, x, p, c))

    def second_x(k, p, at):
        part = rows.at[at, :, c, 1]
        return remote(part, part, second_sent.at[1, k], second_came.at[1, at], (z, p, y, c))

    for copy in local:
        copy.wait()
    for k in range(1, nx):
        p = lax.rem(x + k, nx)
        first_x(k, p, p).wait_recv()
    for k in range(1, ny):
        second_y(k, lax.rem(y + k, ny), y).start()
    for k in range(1, ny):
        p = lax.rem(y + k, ny)
        first_y(k, p, p).wait_recv()
    for k in range(1, nx):
        second_x(k, lax.rem(x + k, nx), x).start()

    lax.fori_loop(cut[0], cut[1], step, 0)

    def core_y(p, of):
        part = rows.at[:, p, of, 0]
        return remote(part, part, core_sent.at[0, p], core_came.at[0, p], other)

    def core_x(p, of):
        part = rows.at[p, :, of, 1]
        return remote(part, part, core_sent.at[1, p], core_came.at[1, p], other)

    core_y(y, c).start()
    core_x(x, c).start()
    for k in range(1, ny):
        p = lax.rem(y + k, ny)
        second_y(k, p, p).wait_recv()
        core_y(p, c).start()
    for k in range(1, nx):
        p = lax.rem(x + k, nx)
        second_x(k, p, p).wait_recv()
        core_x(p, c).start()

    lax.fori_loop(cut[1], steps, step, 0)

    def finish(k, carry):
        p, device = plane_peer(k)
        tile_copy(k, p, device, p).wait_recv()
        list_copy(k, device, p).wait_recv()
        tile_copy(k, p, device, me).wait_send()
        list_copy(k, device, me).wait_send()
        return carry

    lax.fori_loop(1, plane, finish, 0)
    for p in range(ny):
        core_y(p, nc - 1 - c).wait_recv()
        core_y(p, c).wait_send()
    for p in range(nx):
        core_x(p, nc - 1 - c).wait_recv()
        core_x(p, c).wait_send()
    for k in range(1, nx):
        p = lax.rem(x + k, nx)
        first_x(k, p, x).wait_send()
        second_x(k, p, x).wait_send()
    for k in range(1, ny):
        p = lax.rem(y + k, ny)
        first_y(k, p, y).wait_send()
        second_y(k, p, y).wait_send()

    @pl.when(holder != g)
    def _():
        gather(g).wait_send()

    def drain(j, carry):
        @pl.when(origin)
        def _():
            down(hd, j).wait_send()
            up(hd, j).wait_send()

        @pl.when(du < half)
        def _():
            down(hu, j).wait_send()

        @pl.when(jnp.logical_and(jnp.logical_not(origin), dd < half - 1))
        def _():
            up(hd, j).wait_send()

        return carry

    lax.fori_loop(0, chunks, drain, 0)


def bring(panel, lists, tiles):
    sizes = axis_sizes()
    nz, nx, ny, nc = sizes
    group = ny * nc
    plane = nx * group
    blocks, tile, width = panel.shape
    his = nz // group
    span = group * blocks
    anywhere = pl.BlockSpec(memory_space=pl.ANY)
    dma = pltpu.SemaphoreType.DMA
    most = max(nx, ny)
    return pl.pallas_call(
        functools.partial(bring_kernel, sizes),
        out_shape=[
            jax.ShapeDtypeStruct((plane, his, tile, tile), jnp.float32),
            jax.ShapeDtypeStruct((plane,) + lists.shape, jnp.int32),
            jax.ShapeDtypeStruct((his, span, tile, width), jnp.bfloat16),
            jax.ShapeDtypeStruct((nx, ny, nc, blocks, tile, width), jnp.bfloat16),
        ],
        in_specs=[anywhere] * 3,
        out_specs=[anywhere] * 4,
        scratch_shapes=[
            dma((4,)),
            dma((plane,)),
            dma((plane,)),
            dma((plane,)),
            dma((plane,)),
            dma((1,)),
            dma((group,)),
            dma((2, span)),
            dma((2, span)),
            dma((2, most)),
            dma((2, most)),
            dma((2, most)),
            dma((2, most)),
            dma((2, most)),
            dma((2, most)),
        ],
        compiler_params=pltpu.CompilerParams(
            collective_id=1, has_side_effects=True, vmem_limit_bytes=VMEM_LIMIT
        ),
        name="bring",
    )(panel, lists, tiles)


def tiles_kernel(his, blocks, span, step, meta, tiles, cols, rows, fwd, bwd):
    at = pl.program_id(0)

    @pl.when(at == 0)
    def _():
        bwd[...] = jnp.zeros_like(bwd)

    for u in range(step):
        src = at * step + u
        values, panels, picks = [], [], []
        for hi in range(his):
            slot = src * his + hi
            row, col, live = meta[0, slot], meta[1, slot], meta[2, slot]
            t = tiles[u, hi] * live.astype(jnp.float32)
            values.append(t)
            picks.append(row)
            panels.append(cols[hi, col])
            flipped = jnp.concatenate(split2(t.T), axis=1)
            own = rows[u, row]
            got = jnp.dot(
                flipped, jnp.concatenate([own, own], axis=0), preferred_element_type=jnp.float32
            )
            bwd[hi, col] += got
        left = jnp.concatenate(
            [
                jnp.concatenate(
                    [t * (pick == b).astype(jnp.float32) for t, pick in zip(values, picks)], axis=1
                )
                for b in range(blocks)
            ],
            axis=0,
        )
        right = jnp.concatenate(panels, axis=0)
        high, low = split2(left)
        out = jnp.dot(high, right, preferred_element_type=jnp.float32) + jnp.dot(
            low, right, preferred_element_type=jnp.float32
        )
        fwd[u] = out.reshape(fwd.shape[1:])


def tile_products(meta, tiles, cols, rows):
    plane, his, tile, _ = tiles.shape
    blocks, width = rows.shape[1], rows.shape[3]
    span = cols.shape[1]
    step = 4
    return pl.pallas_call(
        functools.partial(tiles_kernel, his, blocks, span, step),
        grid_spec=pltpu.PrefetchScalarGridSpec(
            num_scalar_prefetch=1,
            grid=(plane // step,),
            in_specs=[
                pl.BlockSpec((step, his, tile, tile), lambda i, m: (i, 0, 0, 0)),
                pl.BlockSpec(cols.shape, lambda i, m: (0, 0, 0, 0)),
                pl.BlockSpec((step, blocks, tile, width), lambda i, m: (i, 0, 0, 0)),
            ],
            out_specs=[
                pl.BlockSpec((step, blocks, tile, width), lambda i, m: (i, 0, 0, 0)),
                pl.BlockSpec((his, span, tile, width), lambda i, m: (0, 0, 0, 0)),
            ],
        ),
        out_shape=[
            jax.ShapeDtypeStruct((plane, blocks, tile, width), jnp.float32),
            jax.ShapeDtypeStruct((his, span, tile, width), jnp.float32),
        ],
        compiler_params=pltpu.CompilerParams(vmem_limit_bytes=VMEM_LIMIT),
        name="tile_products",
    )(meta, tiles, cols, rows)


CHUNK = 64
SKEW = 3


def sums_kernel(
    sizes,
    fwd,
    bwd,
    product,
    gram,
    held,
    keep,
    from_core,
    from_x,
    from_y,
    from_below,
    from_above,
    last,
    part,
    got,
    ring,
    whole,
    local_sem,
    chain_sent,
    chain_came,
    last_sent,
    last_came,
    plane_sent,
    plane_came,
    sent,
    came,
):
    nz, nx, ny, nc = sizes
    group = ny * nc
    plane = nx * group
    half = nz // 2
    z, x, y, c = (lax.axis_index(a) for a in AXES)
    g = y * nc + c
    me = x * group + g
    strip = part.shape[0] // plane
    chunks = held.shape[1]
    per_device = last.shape[0]

    def member(p):
        return (z, x, p // nc, lax.rem(p, nc))

    def plane_peer(k):
        p = lax.rem(me + k, plane)
        return p, (z, p // group, lax.rem(p, group) // nc, lax.rem(p, nc))

    def ring_peer(k):
        q = lax.rem(z + k, nz)
        return q, (q, x, y, c)

    def remote(source, target, send_sem, recv_sem, device):
        return pltpu.make_async_remote_copy(
            src_ref=source,
            dst_ref=target,
            send_sem=send_sem,
            recv_sem=recv_sem,
            device_id=device,
            device_id_type=MESH,
        )

    barrier = pltpu.get_barrier_semaphore()

    def greet(peer):
        def body(k, carry):
            pl.semaphore_signal(barrier, inc=1, device_id=peer(k)[1], device_id_type=MESH)
            return carry

        return body

    lax.fori_loop(1, plane, greet(plane_peer), 0)
    lax.fori_loop(1, nz, greet(ring_peer), 0)
    load_held = pltpu.make_async_copy(bwd, held, local_sem.at[0])
    load_keep = pltpu.make_async_copy(fwd.at[:, c], keep, local_sem.at[1])
    load_held.start()
    load_keep.start()
    pl.semaphore_wait(barrier, plane - 1 + nz - 1)

    other = (z, x, y, nc - 1 - c)
    core_copy = remote(
        fwd.at[:, nc - 1 - c], from_core, plane_sent.at[0, 0], plane_came.at[0, 0], other
    )
    core_copy.start()

    d0 = lax.rem(g - z + nz, nz)
    lower = jnp.logical_and(d0 >= 1, d0 <= half)
    hu = jnp.where(lower, 0, 1)
    hd = 1 - hu
    du = jnp.where(lower, d0, lax.rem(d0 + half, nz))
    pu = half - du
    pd = du - 1
    target = du == half
    above = (lax.rem(z + 1, nz), x, y, c)
    below = (lax.rem(z + nz - 1, nz), x, y, c)

    def up(j):
        return remote(
            held.at[hu, j], from_below.at[j], chain_sent.at[0, j], chain_came.at[0, j], above
        )

    def down(j):
        return remote(
            held.at[hd, j], from_above.at[j], chain_sent.at[1, j], chain_came.at[1, j], below
        )

    def scatter(j, at):
        return remote(
            held.at[hd, j], last.at[at], last_sent.at[j], last_came.at[at], member(j // per_device)
        )

    load_held.wait()

    def step(i, carry):
        j = i - SKEW * pu

        @pl.when(jnp.logical_and(j >= 0, j < chunks))
        def _():
            @pl.when(pu > 0)
            def _():
                up(j).wait_recv()
                held[hu, j] += from_below[j]

            up(j).start()

        jd = i - SKEW * pd

        @pl.when(jnp.logical_and(jnp.logical_not(target), jnp.logical_and(jd >= 0, jd < chunks)))
        def _():
            @pl.when(pd > 0)
            def _():
                down(jd).wait_recv()
                held[hd, jd] += from_above[jd]

            down(jd).start()

        jt = i - SKEW * half

        @pl.when(jnp.logical_and(target, jnp.logical_and(jt >= 0, jt < chunks)))
        def _():
            up(jt).wait_recv()
            down(jt).wait_recv()
            held[hd, jt] += from_below[jt] + from_above[jt]
            at = lax.rem(jt, per_device)

            @pl.when(jt // per_device == g)
            def _():
                last[at] = held[hd, jt]

            @pl.when(jt // per_device != g)
            def _():
                scatter(jt, at).start()

        return carry

    steps = chunks + SKEW * half
    cut = (steps // 5, (3 * steps) // 4)
    lax.fori_loop(0, cut[0], step, 0)

    load_keep.wait()
    core_copy.wait()

    def x_copy(k):
        p = lax.rem(x + k, nx)
        return remote(
            keep.at[pl.ds(p * ny, ny)],
            from_x.at[x],
            plane_sent.at[1, k],
            plane_came.at[1, x],
            (z, p, y, c),
        )

    def x_source(k):
        p = lax.rem(x + k, nx)
        return p, remote(
            from_x.at[p], from_x.at[p], plane_sent.at[1, k], plane_came.at[1, p], (z, p, y, c)
        )

    for k in range(1, nx + 1):
        p = lax.rem(x + k, nx)

        def add_core(i, carry, p=p):
            keep[p * ny + i] += from_core[p * ny + i]
            return carry

        lax.fori_loop(0, ny, add_core, 0)
        if k < nx:
            x_copy(k).start()

    lax.fori_loop(cut[0], cut[1], step, 0)

    for k in range(1, nx):
        p, copy = x_source(k)
        copy.wait_recv()

        def add_x(i, carry, p=p):
            keep[x * ny + i] += from_x[p, i]
            return carry

        lax.fori_loop(0, ny, add_x, 0)

    def y_copy(k):
        p = lax.rem(y + k, ny)
        return remote(
            keep.at[x * ny + p],
            from_y.at[y],
            plane_sent.at[2, k],
            plane_came.at[2, y],
            (z, x, p, c),
        )

    for k in range(1, ny):
        y_copy(k).start()

    lax.fori_loop(cut[1], steps, step, 0)

    total = keep[x * ny + y]
    for k in range(1, ny):
        p = lax.rem(y + k, ny)
        remote(
            from_y.at[p], from_y.at[p], plane_sent.at[2, k], plane_came.at[2, p], (z, x, p, c)
        ).wait_recv()
        total = total + from_y[p]
    holder = lax.rem(z, group)

    @pl.when(holder != g)
    def _():
        for at in range(per_device):
            scatter(at, at).wait_recv()

    total = total + last[...].reshape(total.shape)
    product[...] = total
    part[...] = lax.dot_general(
        total, total, (((0,), (0,)), ((), ())), precision=HIGHEST, preferred_element_type=jnp.float32
    )

    def rows_of(p):
        return pl.ds(pl.multiple_of(p * strip, strip), strip)

    def exchange(count, peer, stage, mine, source, target_of):
        def copy(k, p, device):
            return remote(
                source(p), target_of(mine), sent.at[stage, k], came.at[stage, mine], device
            )

        def start(k, carry):
            p, device = peer(k)
            copy(k, p, device).start()
            return carry

        def finish(k, carry):
            p, device = peer(k)
            copy(k, p, device).wait_send()
            remote(
                target_of(p), target_of(p), sent.at[stage, k], came.at[stage, p], device
            ).wait_recv()
            return carry

        lax.fori_loop(1, count, start, 0)
        lax.fori_loop(1, count, finish, 0)

    exchange(plane, plane_peer, 0, me, lambda p: part.at[rows_of(p)], lambda p: got.at[p])
    strip_sum = part[rows_of(me)]
    for k in range(1, plane):
        strip_sum = strip_sum + got[lax.rem(me + k, plane)]
    ring[z] = strip_sum
    exchange(nz, ring_peer, 1, z, lambda p: ring.at[z], lambda p: ring.at[p])
    strip_sum = ring[0]
    for k in range(1, nz):
        strip_sum = strip_sum + ring[k]
    whole[rows_of(me)] = strip_sum
    exchange(
        plane, plane_peer, 2, me, lambda p: whole.at[rows_of(me)], lambda p: whole.at[rows_of(p)]
    )
    gram[...] = whole[...]

    for k in range(1, nx):
        x_copy(k).wait_send()
    for k in range(1, ny):
        y_copy(k).wait_send()

    def drain(j, carry):
        up(j).wait_send()

        @pl.when(jnp.logical_not(target))
        def _():
            down(j).wait_send()

        @pl.when(jnp.logical_and(target, j // per_device != g))
        def _():
            scatter(j, lax.rem(j, per_device)).wait_send()

        return carry

    lax.fori_loop(0, chunks, drain, 0)


def device_sums(fwd, bwd):
    sizes = axis_sizes()
    nz, nx, ny, nc = sizes
    group = ny * nc
    plane = nx * group
    _, rows, width = fwd.shape
    strip = width // plane
    most = max(plane, nz)
    chunks = group * rows // CHUNK
    fwd = fwd.reshape(nx * ny, nc, rows, width)
    bwd = bwd.reshape(2, chunks, CHUNK, width)
    vmem = pl.BlockSpec(memory_space=pltpu.VMEM)
    anywhere = pl.BlockSpec(memory_space=pl.ANY)

    def buffer(*shape):
        return pltpu.VMEM(shape, jnp.float32)

    dma = pltpu.SemaphoreType.DMA
    return pl.pallas_call(
        functools.partial(sums_kernel, sizes),
        out_shape=[
            jax.ShapeDtypeStruct((rows, width), jnp.float32),
            jax.ShapeDtypeStruct((width, width), jnp.float32),
        ],
        in_specs=[anywhere, anywhere],
        out_specs=[vmem, vmem],
        scratch_shapes=[
            buffer(2, chunks, CHUNK, width),
            buffer(nx * ny, rows, width),
            buffer(nx * ny, rows, width),
            buffer(nx, ny, rows, width),
            buffer(ny, rows, width),
            buffer(chunks, CHUNK, width),
            buffer(chunks, CHUNK, width),
            buffer(rows // CHUNK, CHUNK, width),
            buffer(width, width),
            buffer(plane, strip, width),
            buffer(nz, strip, width),
            buffer(width, width),
            dma((2,)),
            dma((2, chunks)),
            dma((2, chunks)),
            dma((chunks,)),
            dma((rows // CHUNK,)),
            dma((3, max(nx, ny))),
            dma((3, max(nx, ny))),
            dma((3, most)),
            dma((3, most)),
        ],
        compiler_params=pltpu.CompilerParams(
            collective_id=0, has_side_effects=True, vmem_limit_bytes=VMEM_LIMIT
        ),
        name="device_sums",
    )(fwd, bwd)


def dot_high(a, b, dims):
    return lax.dot_general(
        a, b, (dims, ((), ())), precision=HIGHEST, preferred_element_type=jnp.float32
    )


def inverse_factor(a):
    n = a.shape[0]
    sub = 8
    lanes = lax.broadcasted_iota(jnp.int32, (sub, n), 1)
    subs = lax.broadcasted_iota(jnp.int32, (sub, n), 0)
    left = [a[i * sub : (i + 1) * sub] for i in range(n // sub)]
    right = [(lanes == subs + i * sub).astype(jnp.float32) for i in range(n // sub)]
    for j in range(n):
        t0, s = divmod(j, sub)
        row = left[t0][s : s + 1]
        inv = 1.0 / row[:, j : j + 1]
        wrow = right[t0][s : s + 1]
        scaled = row * inv
        wscaled = wrow * inv
        for t in range(t0, n // sub):
            col = left[t][:, j : j + 1]
            if t == t0:
                col = jnp.where(subs[:, :1] > s, col, 0.0)
            left[t] = left[t] - col * scaled
            right[t] = right[t] - col * wscaled
    out = []
    for t in range(n // sub):
        d = jnp.sum(jnp.where(lanes == subs + t * sub, left[t], 0.0), axis=1, keepdims=True)
        out.append(right[t] * lax.rsqrt(d))
    return jnp.concatenate(out, axis=0)


def basis_kernel(scale, gram, product, basis):
    n = gram.shape[0]
    h = n // 2
    g11 = gram[:h, :h] * scale
    g21 = gram[h:, :h] * scale
    g22 = gram[h:, h:] * scale
    w11 = inverse_factor(g11)
    l21 = dot_high(g21, w11, ((1,), (1,)))
    w22 = inverse_factor(g22 - dot_high(l21, l21, ((1,), (1,))))
    w21 = -dot_high(w22, dot_high(l21, w11, ((1,), (0,))), ((1,), (0,)))
    first = product[:, :h]
    basis[:, :h] = dot_high(first, w11, ((1,), (1,)))
    basis[:, h:] = dot_high(first, w21, ((1,), (1,))) + dot_high(
        product[:, h:], w22, ((1,), (1,))
    )


def new_basis(gram, product, nodes):
    vmem = pl.BlockSpec(memory_space=pltpu.VMEM)
    return pl.pallas_call(
        functools.partial(basis_kernel, 1.0 / nodes),
        out_shape=jax.ShapeDtypeStruct(product.shape, jnp.float32),
        in_specs=[vmem, vmem],
        out_specs=vmem,
        compiler_params=pltpu.CompilerParams(vmem_limit_bytes=VMEM_LIMIT),
        name="new_basis",
    )(gram, product)


def shards(panel, lists, tiles):
    nz, nx, ny, nc = axis_sizes()
    group = ny * nc
    plane = nx * group
    tile = tiles.shape[1]
    width = panel.shape[1]
    blocks = panel.shape[0] // tile
    nodes = panel.shape[0] * nz * plane
    his = nz // group
    own = panel.reshape(blocks, tile, width)
    here, meta, cols, rows = bring(
        own,
        jnp.pad(lists, ((0, 8 - 3), (0, 128 - lists.shape[1] % 128))),
        tiles.reshape(his, group * nx, tile, tile),
    )
    place = (lax.axis_index("y") * nc + lax.axis_index("core")) * nx + lax.axis_index("x")
    meta = meta[:, :3, : lists.shape[1]].reshape(plane, 3, his, group * nx)
    meta = lax.dynamic_index_in_dim(meta, place, 3, keepdims=False)
    meta = meta.transpose(1, 0, 2).reshape(3, plane * his)
    rows = rows.reshape(plane, blocks, tile, width)
    fwd, bwd = tile_products(meta, here, cols, rows)
    product, gram = device_sums(
        fwd.reshape(plane, blocks * tile, width), bwd.reshape(his, group * blocks * tile, width)
    )
    return new_basis(gram, product, nodes)


def solution(mesh):
    sizes = mesh.devices.shape
    nx, ny, nc = grid_of(sizes)
    fine = Mesh(mesh.devices.reshape(sizes[0] // nx, nx, ny, nc), AXES)
    return jax.shard_map(
        shards,
        mesh=fine,
        in_specs=(P(AXES, None), P(None, AXES), P(AXES, None, None)),
        out_specs=P(AXES, None),
        check_vma=False,
    )


def grid_of(sizes):
    return (4, 4, 2) if sizes == (64, 8) else (2, 1, 2)
```

```python
import functools

import jax
import jax.numpy as jnp
from jax import lax
from jax.experimental import pallas as pl
from jax.experimental.pallas import tpu as pltpu
from jax.sharding import Mesh, PartitionSpec as P

HIGHEST = lax.Precision.HIGHEST
MESH = pl.DeviceIdType.MESH
VMEM_LIMIT = 56 * 1024 * 1024
AXES = ("z", "x", "y", "core")


def axis_sizes():
    return tuple(lax.axis_size(a) for a in AXES)


def split2(t):
    high = t.astype(jnp.bfloat16)
    low = (t - high.astype(jnp.float32)).astype(jnp.bfloat16)
    return high, low


CODE_TOP = 32767.0
PASS = 3


def bring_kernel(
    sizes,
    panel,
    lists,
    tiles,
    here,
    meta,
    cols,
    rows,
    stage,
    coded,
    message,
    local_sem,
    tile_sent,
    tile_came,
    list_sent,
    list_came,
    gather_sent,
    gather_came,
    chain_sent,
    chain_came,
    first_sent,
    first_came,
    second_sent,
    second_came,
    core_sent,
    core_came,
):
    nz, nx, ny, nc = sizes
    group = ny * nc
    plane = nx * group
    half = nz // 2
    z, x, y, c = (lax.axis_index(a) for a in AXES)
    g = y * nc + c
    me = x * group + g
    blocks = panel.shape[0]
    chunks = cols.shape[1]

    def member(p):
        return (z, x, p // nc, lax.rem(p, nc))

    def plane_peer(k):
        across = lax.rem(k, nx)
        px = lax.rem(x + across, nx)
        py = lax.rem(y + lax.rem(k // nx, ny) + across, ny)
        pc = lax.rem(c + k // (nx * ny), nc)
        return px * group + py * nc + pc, (z, px, py, pc)

    def remote(source, target, send_sem, recv_sem, device):
        return pltpu.make_async_remote_copy(
            src_ref=source,
            dst_ref=target,
            send_sem=send_sem,
            recv_sem=recv_sem,
            device_id=device,
            device_id_type=MESH,
        )

    above = (lax.rem(z + 1, nz), x, y, c)
    below = (lax.rem(z + nz - 1, nz), x, y, c)
    other = (z, x, y, nc - 1 - c)

    barrier = pltpu.get_barrier_semaphore()

    def greet(k, carry):
        pl.semaphore_signal(barrier, inc=1, device_id=plane_peer(k)[1], device_id_type=MESH)
        return carry

    lax.fori_loop(1, plane, greet, 0)
    for device in (above, below):
        pl.semaphore_signal(barrier, inc=1, device_id=device, device_id_type=MESH)

    holder = lax.rem(z, group)
    his = z // group
    local = [
        pltpu.make_async_copy(panel, rows.at[x, y, c], local_sem.at[0]),
        pltpu.make_async_copy(coded.at[me], here.at[me], local_sem.at[1]),
        pltpu.make_async_copy(message.at[me], meta.at[me], local_sem.at[2]),
    ]
    load = pltpu.make_async_copy(tiles, stage, local_sem.at[4])
    load.start()
    to_cols = pltpu.make_async_copy(
        panel, cols.at[his, pl.ds(g * blocks, blocks)], local_sem.at[3]
    )
    local[0].start()

    @pl.when(holder == g)
    def _():
        to_cols.start()

    pl.semaphore_wait(barrier, plane - 1 + 2)

    def gather(p):
        return remote(
            panel,
            cols.at[his, pl.ds(p * blocks, blocks)],
            gather_sent.at[0],
            gather_came.at[p],
            member(holder),
        )

    @pl.when(holder != g)
    def _():
        gather(g).start()

    def first_x(k, p, at):
        return remote(
            panel.at[0], rows.at[at, y, c, 0], first_sent.at[0, k], first_came.at[0, at], (z, p, y, c)
        )

    def first_y(k, p, at):
        return remote(
            panel.at[1], rows.at[x, at, c, 1], first_sent.at[1, k], first_came.at[1, at], (z, x, p, c)
        )

    for k in range(1, nx):
        first_x(k, lax.rem(x + k, nx), x).start()
    for k in range(1, ny):
        first_y(k, lax.rem(y + k, ny), y).start()

    def tile_copy(k, p, device, at):
        return remote(coded.at[p], here.at[at], tile_sent.at[k], tile_came.at[at], device)

    def list_copy(k, p, device, at):
        return remote(message.at[p], meta.at[at], list_sent.at[k], list_came.at[at], device)

    def code(p):
        to = lax.rem(p, group) * nx + p // group
        entry = lists[p]
        for h in range(tiles.shape[0]):
            t = stage[h, to]
            top = jnp.maximum(jnp.max(jnp.abs(t), axis=0, keepdims=True), 1e-30)
            coded[p, h] = jnp.round(t * (CODE_TOP / top)).astype(jnp.int32).astype(jnp.int16)
            line = lax.broadcasted_iota(jnp.int32, entry.shape, 0)
            entry = jnp.where(line == h, top * (1.0 / CODE_TOP), entry)
        message[p] = entry

    def start_tiles(k, carry):
        p, device = plane_peer(k)
        code(p)
        list_copy(k, p, device, me).start()
        tile_copy(k, p, device, me).start()
        return carry

    load.wait()
    lax.fori_loop(1, plane, start_tiles, 0)
    code(me)
    local[1].start()
    local[2].start()

    d0 = lax.rem(g - z + nz, nz)
    lower = jnp.logical_and(d0 >= 1, d0 <= half)
    hu = jnp.where(lower, 0, 1)
    hd = 1 - hu
    du = jnp.where(lower, d0, lax.rem(d0 + half, nz))
    dd = half - du
    origin = du == half

    def down(h, j):
        return remote(
            cols.at[h, j], cols.at[h, j], chain_sent.at[0, j], chain_came.at[0, j], below
        )

    def up(h, j):
        return remote(
            cols.at[h, j], cols.at[h, j], chain_sent.at[1, j], chain_came.at[1, j], above
        )

    def in_turn(j):
        return lax.rem(g + j // blocks, group) * blocks + lax.rem(j, blocks)

    @pl.when(origin)
    def _():
        to_cols.wait()
        for m in range(group):
            if m > 0:
                gather(lax.rem(g + m, group)).wait_recv()
            for b in range(blocks):
                down(hd, in_turn(m * blocks + b)).start()
                up(hd, in_turn(m * blocks + b)).start()

    def step(i, carry):
        j = i - PASS * (du - 1)

        @pl.when(jnp.logical_and(j >= 0, j < chunks))
        def _():
            down(hu, in_turn(j)).wait_recv()

            @pl.when(du < half)
            def _():
                down(hu, in_turn(j)).start()

        ju = i - PASS * (dd - 1)

        @pl.when(jnp.logical_and(jnp.logical_not(origin), jnp.logical_and(ju >= 0, ju < chunks)))
        def _():
            up(hd, in_turn(ju)).wait_recv()

            @pl.when(dd < half - 1)
            def _():
                up(hd, in_turn(ju)).start()

        return carry

    steps = chunks + PASS * (half - 1)
    cut = (steps // 3, (2 * steps) // 3)
    lax.fori_loop(0, cut[0], step, 0)

    def second_y(k, p, at):
        part = rows.at[:, at, c, 0]
        return remote(part, part, second_sent.at[0, k], second_came.at[0, at], (z, x, p, c))

    def second_x(k, p, at):
        part = rows.at[at, :, c, 1]
        return remote(part, part, second_sent.at[1, k], second_came.at[1, at], (z, p, y, c))

    for copy in local:
        copy.wait()
    for k in range(1, nx):
        p = lax.rem(x + k, nx)
        first_x(k, p, p).wait_recv()
    for k in range(1, ny):
        second_y(k, lax.rem(y + k, ny), y).start()
    for k in range(1, ny):
        p = lax.rem(y + k, ny)
        first_y(k, p, p).wait_recv()
    for k in range(1, nx):
        second_x(k, lax.rem(x + k, nx), x).start()

    lax.fori_loop(cut[0], cut[1], step, 0)

    def core_y(p, of):
        part = rows.at[:, p, of, 0]
        return remote(part, part, core_sent.at[0, p], core_came.at[0, p], other)

    def core_x(p, of):
        part = rows.at[p, :, of, 1]
        return remote(part, part, core_sent.at[1, p], core_came.at[1, p], other)

    core_y(y, c).start()
    core_x(x, c).start()
    for k in range(1, ny):
        p = lax.rem(y + k, ny)
        second_y(k, p, p).wait_recv()
        core_y(p, c).start()
    for k in range(1, nx):
        p = lax.rem(x + k, nx)
        second_x(k, p, p).wait_recv()
        core_x(p, c).start()

    lax.fori_loop(cut[1], steps, step, 0)

    def finish(k, carry):
        p, device = plane_peer(k)
        tile_copy(k, p, device, p).wait_recv()
        list_copy(k, p, device, p).wait_recv()
        tile_copy(k, p, device, me).wait_send()
        list_copy(k, p, device, me).wait_send()
        return carry

    lax.fori_loop(1, plane, finish, 0)
    for p in range(ny):
        core_y(p, nc - 1 - c).wait_recv()
        core_y(p, c).wait_send()
    for p in range(nx):
        core_x(p, nc - 1 - c).wait_recv()
        core_x(p, c).wait_send()
    for k in range(1, nx):
        p = lax.rem(x + k, nx)
        first_x(k, p, x).wait_send()
        second_x(k, p, x).wait_send()
    for k in range(1, ny):
        p = lax.rem(y + k, ny)
        first_y(k, p, y).wait_send()
        second_y(k, p, y).wait_send()

    @pl.when(holder != g)
    def _():
        gather(g).wait_send()

    def drain(j, carry):
        @pl.when(origin)
        def _():
            down(hd, j).wait_send()
            up(hd, j).wait_send()

        @pl.when(du < half)
        def _():
            down(hu, j).wait_send()

        @pl.when(jnp.logical_and(jnp.logical_not(origin), dd < half - 1))
        def _():
            up(hd, j).wait_send()

        return carry

    lax.fori_loop(0, chunks, drain, 0)


def bring(panel, lists, tiles):
    sizes = axis_sizes()
    nz, nx, ny, nc = sizes
    group = ny * nc
    plane = nx * group
    blocks, tile, width = panel.shape
    his = nz // group
    span = group * blocks
    anywhere = pl.BlockSpec(memory_space=pl.ANY)
    dma = pltpu.SemaphoreType.DMA
    most = max(nx, ny)
    return pl.pallas_call(
        functools.partial(bring_kernel, sizes),
        out_shape=[
            jax.ShapeDtypeStruct((plane, his, tile, tile), jnp.int16),
            jax.ShapeDtypeStruct(lists.shape, jnp.float32),
            jax.ShapeDtypeStruct((his, span, tile, width), jnp.bfloat16),
            jax.ShapeDtypeStruct((nx, ny, nc, blocks, tile, width), jnp.bfloat16),
        ],
        in_specs=[anywhere, pl.BlockSpec(memory_space=pltpu.VMEM), anywhere],
        out_specs=[anywhere] * 4,
        scratch_shapes=[
            pltpu.VMEM(tiles.shape, jnp.float32),
            pltpu.VMEM((plane, his, tile, tile), jnp.int16),
            pltpu.VMEM(lists.shape, jnp.float32),
            dma((5,)),
            dma((plane,)),
            dma((plane,)),
            dma((plane,)),
            dma((plane,)),
            dma((1,)),
            dma((group,)),
            dma((2, span)),
            dma((2, span)),
            dma((2, most)),
            dma((2, most)),
            dma((2, most)),
            dma((2, most)),
            dma((2, most)),
            dma((2, most)),
        ],
        compiler_params=pltpu.CompilerParams(
            collective_id=1, has_side_effects=True, vmem_limit_bytes=VMEM_LIMIT
        ),
        name="bring",
    )(panel, lists, tiles)


def tiles_kernel(his, blocks, span, step, meta, tiles, scales, cols, rows, fwd, bwd):
    at = pl.program_id(0)

    @pl.when(at == 0)
    def _():
        bwd[...] = jnp.zeros_like(bwd)

    for u in range(step):
        src = at * step + u
        values, panels, picks = [], [], []
        for hi in range(his):
            slot = src * his + hi
            row, col, live = meta[0, slot], meta[1, slot], meta[2, slot]
            scale = scales[u, hi : hi + 1] * live.astype(jnp.float32)
            t = tiles[u, hi].astype(jnp.int32).astype(jnp.float32) * scale
            values.append(t)
            picks.append(row)
            panels.append(cols[hi, col])
            flipped = jnp.concatenate(split2(t.T), axis=1)
            own = rows[u, row]
            got = jnp.dot(
                flipped, jnp.concatenate([own, own], axis=0), preferred_element_type=jnp.float32
            )
            bwd[hi, col] += got
        left = jnp.concatenate(
            [
                jnp.concatenate(
                    [t * (pick == b).astype(jnp.float32) for t, pick in zip(values, picks)], axis=1
                )
                for b in range(blocks)
            ],
            axis=0,
        )
        right = jnp.concatenate(panels, axis=0)
        high, low = split2(left)
        out = jnp.dot(high, right, preferred_element_type=jnp.float32) + jnp.dot(
            low, right, preferred_element_type=jnp.float32
        )
        fwd[u] = out.reshape(fwd.shape[1:])


def tile_products(meta, tiles, scales, cols, rows):
    plane, his, tile, _ = tiles.shape
    blocks, width = rows.shape[1], rows.shape[3]
    span = cols.shape[1]
    step = 4
    return pl.pallas_call(
        functools.partial(tiles_kernel, his, blocks, span, step),
        grid_spec=pltpu.PrefetchScalarGridSpec(
            num_scalar_prefetch=1,
            grid=(plane // step,),
            in_specs=[
                pl.BlockSpec((step, his, tile, tile), lambda i, m: (i, 0, 0, 0)),
                pl.BlockSpec((step,) + scales.shape[1:], lambda i, m: (i, 0, 0)),
                pl.BlockSpec(cols.shape, lambda i, m: (0, 0, 0, 0)),
                pl.BlockSpec((step, blocks, tile, width), lambda i, m: (i, 0, 0, 0)),
            ],
            out_specs=[
                pl.BlockSpec((step, blocks, tile, width), lambda i, m: (i, 0, 0, 0)),
                pl.BlockSpec((his, span, tile, width), lambda i, m: (0, 0, 0, 0)),
            ],
        ),
        out_shape=[
            jax.ShapeDtypeStruct((plane, blocks, tile, width), jnp.float32),
            jax.ShapeDtypeStruct((his, span, tile, width), jnp.float32),
        ],
        compiler_params=pltpu.CompilerParams(vmem_limit_bytes=VMEM_LIMIT),
        name="tile_products",
    )(meta, tiles, scales, cols, rows)


CHUNK = 64
SKEW = 3


def sums_kernel(
    sizes,
    fwd,
    bwd,
    product,
    gram,
    held,
    keep,
    from_core,
    from_x,
    from_y,
    from_below,
    from_above,
    last,
    part,
    got,
    ring,
    whole,
    local_sem,
    chain_sent,
    chain_came,
    last_sent,
    last_came,
    plane_sent,
    plane_came,
    sent,
    came,
):
    nz, nx, ny, nc = sizes
    group = ny * nc
    plane = nx * group
    half = nz // 2
    z, x, y, c = (lax.axis_index(a) for a in AXES)
    g = y * nc + c
    me = x * group + g
    strip = part.shape[0] // plane
    chunks = held.shape[1]
    per_device = last.shape[0]

    def member(p):
        return (z, x, p // nc, lax.rem(p, nc))

    def plane_peer(k):
        p = lax.rem(me + k, plane)
        return p, (z, p // group, lax.rem(p, group) // nc, lax.rem(p, nc))

    def ring_peer(k):
        q = lax.rem(z + k, nz)
        return q, (q, x, y, c)

    def remote(source, target, send_sem, recv_sem, device):
        return pltpu.make_async_remote_copy(
            src_ref=source,
            dst_ref=target,
            send_sem=send_sem,
            recv_sem=recv_sem,
            device_id=device,
            device_id_type=MESH,
        )

    barrier = pltpu.get_barrier_semaphore()

    def greet(peer):
        def body(k, carry):
            pl.semaphore_signal(barrier, inc=1, device_id=peer(k)[1], device_id_type=MESH)
            return carry

        return body

    lax.fori_loop(1, plane, greet(plane_peer), 0)
    lax.fori_loop(1, nz, greet(ring_peer), 0)
    load_held = pltpu.make_async_copy(bwd, held, local_sem.at[0])
    load_keep = pltpu.make_async_copy(fwd.at[:, c], keep, local_sem.at[1])
    load_held.start()
    load_keep.start()
    pl.semaphore_wait(barrier, plane - 1 + nz - 1)

    other = (z, x, y, nc - 1 - c)
    core_copy = remote(
        fwd.at[:, nc - 1 - c], from_core, plane_sent.at[0, 0], plane_came.at[0, 0], other
    )
    core_copy.start()

    d0 = lax.rem(g - z + nz, nz)
    lower = jnp.logical_and(d0 >= 1, d0 <= half)
    hu = jnp.where(lower, 0, 1)
    hd = 1 - hu
    du = jnp.where(lower, d0, lax.rem(d0 + half, nz))
    pu = half - du
    pd = du - 1
    target = du == half
    above = (lax.rem(z + 1, nz), x, y, c)
    below = (lax.rem(z + nz - 1, nz), x, y, c)

    def up(j):
        return remote(
            held.at[hu, j], from_below.at[j], chain_sent.at[0, j], chain_came.at[0, j], above
        )

    def down(j):
        return remote(
            held.at[hd, j], from_above.at[j], chain_sent.at[1, j], chain_came.at[1, j], below
        )

    def scatter(j, at):
        return remote(
            held.at[hd, j], last.at[at], last_sent.at[j], last_came.at[at], member(j // per_device)
        )

    load_held.wait()

    def step(i, carry):
        j = i - SKEW * pu

        @pl.when(jnp.logical_and(j >= 0, j < chunks))
        def _():
            @pl.when(pu > 0)
            def _():
                up(j).wait_recv()
                held[hu, j] += from_below[j]

            up(j).start()

        jd = i - SKEW * pd

        @pl.when(jnp.logical_and(jnp.logical_not(target), jnp.logical_and(jd >= 0, jd < chunks)))
        def _():
            @pl.when(pd > 0)
            def _():
                down(jd).wait_recv()
                held[hd, jd] += from_above[jd]

            down(jd).start()

        jt = i - SKEW * half

        @pl.when(jnp.logical_and(target, jnp.logical_and(jt >= 0, jt < chunks)))
        def _():
            up(jt).wait_recv()
            down(jt).wait_recv()
            held[hd, jt] += from_below[jt] + from_above[jt]
            at = lax.rem(jt, per_device)

            @pl.when(jt // per_device == g)
            def _():
                last[at] = held[hd, jt]

            @pl.when(jt // per_device != g)
            def _():
                scatter(jt, at).start()

        return carry

    steps = chunks + SKEW * half
    cut = (steps // 5, (3 * steps) // 4)
    lax.fori_loop(0, cut[0], step, 0)

    load_keep.wait()
    core_copy.wait()

    def x_copy(k):
        p = lax.rem(x + k, nx)
        return remote(
            keep.at[pl.ds(p * ny, ny)],
            from_x.at[x],
            plane_sent.at[1, k],
            plane_came.at[1, x],
            (z, p, y, c),
        )

    def x_source(k):
        p = lax.rem(x + k, nx)
        return p, remote(
            from_x.at[p], from_x.at[p], plane_sent.at[1, k], plane_came.at[1, p], (z, p, y, c)
        )

    for k in range(1, nx + 1):
        p = lax.rem(x + k, nx)

        def add_core(i, carry, p=p):
            keep[p * ny + i] += from_core[p * ny + i]
            return carry

        lax.fori_loop(0, ny, add_core, 0)
        if k < nx:
            x_copy(k).start()

    lax.fori_loop(cut[0], cut[1], step, 0)

    for k in range(1, nx):
        p, copy = x_source(k)
        copy.wait_recv()

        def add_x(i, carry, p=p):
            keep[x * ny + i] += from_x[p, i]
            return carry

        lax.fori_loop(0, ny, add_x, 0)

    def y_copy(k):
        p = lax.rem(y + k, ny)
        return remote(
            keep.at[x * ny + p],
            from_y.at[y],
            plane_sent.at[2, k],
            plane_came.at[2, y],
            (z, x, p, c),
        )

    for k in range(1, ny):
        y_copy(k).start()

    lax.fori_loop(cut[1], steps, step, 0)

    total = keep[x * ny + y]
    for k in range(1, ny):
        p = lax.rem(y + k, ny)
        remote(
            from_y.at[p], from_y.at[p], plane_sent.at[2, k], plane_came.at[2, p], (z, x, p, c)
        ).wait_recv()
        total = total + from_y[p]
    holder = lax.rem(z, group)

    @pl.when(holder != g)
    def _():
        for at in range(per_device):
            scatter(at, at).wait_recv()

    total = total + last[...].reshape(total.shape)
    product[...] = total
    part[...] = lax.dot_general(
        total, total, (((0,), (0,)), ((), ())), precision=HIGHEST, preferred_element_type=jnp.float32
    )

    def rows_of(p):
        return pl.ds(pl.multiple_of(p * strip, strip), strip)

    def exchange(count, peer, stage, mine, source, target_of):
        def copy(k, p, device):
            return remote(
                source(p), target_of(mine), sent.at[stage, k], came.at[stage, mine], device
            )

        def start(k, carry):
            p, device = peer(k)
            copy(k, p, device).start()
            return carry

        def finish(k, carry):
            p, device = peer(k)
            copy(k, p, device).wait_send()
            remote(
                target_of(p), target_of(p), sent.at[stage, k], came.at[stage, p], device
            ).wait_recv()
            return carry

        lax.fori_loop(1, count, start, 0)
        lax.fori_loop(1, count, finish, 0)

    exchange(plane, plane_peer, 0, me, lambda p: part.at[rows_of(p)], lambda p: got.at[p])
    strip_sum = part[rows_of(me)]
    for k in range(1, plane):
        strip_sum = strip_sum + got[lax.rem(me + k, plane)]
    ring[z] = strip_sum
    exchange(nz, ring_peer, 1, z, lambda p: ring.at[z], lambda p: ring.at[p])
    strip_sum = ring[0]
    for k in range(1, nz):
        strip_sum = strip_sum + ring[k]
    whole[rows_of(me)] = strip_sum
    exchange(
        plane, plane_peer, 2, me, lambda p: whole.at[rows_of(me)], lambda p: whole.at[rows_of(p)]
    )
    gram[...] = whole[...]

    for k in range(1, nx):
        x_copy(k).wait_send()
    for k in range(1, ny):
        y_copy(k).wait_send()

    def drain(j, carry):
        up(j).wait_send()

        @pl.when(jnp.logical_not(target))
        def _():
            down(j).wait_send()

        @pl.when(jnp.logical_and(target, j // per_device != g))
        def _():
            scatter(j, lax.rem(j, per_device)).wait_send()

        return carry

    lax.fori_loop(0, chunks, drain, 0)


def device_sums(fwd, bwd):
    sizes = axis_sizes()
    nz, nx, ny, nc = sizes
    group = ny * nc
    plane = nx * group
    _, rows, width = fwd.shape
    strip = width // plane
    most = max(plane, nz)
    chunks = group * rows // CHUNK
    fwd = fwd.reshape(nx * ny, nc, rows, width)
    bwd = bwd.reshape(2, chunks, CHUNK, width)
    vmem = pl.BlockSpec(memory_space=pltpu.VMEM)
    anywhere = pl.BlockSpec(memory_space=pl.ANY)

    def buffer(*shape):
        return pltpu.VMEM(shape, jnp.float32)

    dma = pltpu.SemaphoreType.DMA
    return pl.pallas_call(
        functools.partial(sums_kernel, sizes),
        out_shape=[
            jax.ShapeDtypeStruct((rows, width), jnp.float32),
            jax.ShapeDtypeStruct((width, width), jnp.float32),
        ],
        in_specs=[anywhere, anywhere],
        out_specs=[vmem, vmem],
        scratch_shapes=[
            buffer(2, chunks, CHUNK, width),
            buffer(nx * ny, rows, width),
            buffer(nx * ny, rows, width),
            buffer(nx, ny, rows, width),
            buffer(ny, rows, width),
            buffer(chunks, CHUNK, width),
            buffer(chunks, CHUNK, width),
            buffer(rows // CHUNK, CHUNK, width),
            buffer(width, width),
            buffer(plane, strip, width),
            buffer(nz, strip, width),
            buffer(width, width),
            dma((2,)),
            dma((2, chunks)),
            dma((2, chunks)),
            dma((chunks,)),
            dma((rows // CHUNK,)),
            dma((3, max(nx, ny))),
            dma((3, max(nx, ny))),
            dma((3, most)),
            dma((3, most)),
        ],
        compiler_params=pltpu.CompilerParams(
            collective_id=0, has_side_effects=True, vmem_limit_bytes=VMEM_LIMIT
        ),
        name="device_sums",
    )(fwd, bwd)


def dot_high(a, b, dims):
    return lax.dot_general(
        a, b, (dims, ((), ())), precision=HIGHEST, preferred_element_type=jnp.float32
    )


def inverse_factor(a):
    n = a.shape[0]
    sub = 8
    lanes = lax.broadcasted_iota(jnp.int32, (sub, n), 1)
    subs = lax.broadcasted_iota(jnp.int32, (sub, n), 0)
    left = [a[i * sub : (i + 1) * sub] for i in range(n // sub)]
    right = [(lanes == subs + i * sub).astype(jnp.float32) for i in range(n // sub)]
    for j in range(n):
        t0, s = divmod(j, sub)
        row = left[t0][s : s + 1]
        inv = 1.0 / row[:, j : j + 1]
        wrow = right[t0][s : s + 1]
        scaled = row * inv
        wscaled = wrow * inv
        for t in range(t0, n // sub):
            col = left[t][:, j : j + 1]
            if t == t0:
                col = jnp.where(subs[:, :1] > s, col, 0.0)
            left[t] = left[t] - col * scaled
            right[t] = right[t] - col * wscaled
    out = []
    for t in range(n // sub):
        d = jnp.sum(jnp.where(lanes == subs + t * sub, left[t], 0.0), axis=1, keepdims=True)
        out.append(right[t] * lax.rsqrt(d))
    return jnp.concatenate(out, axis=0)


def eliminated(gram, scale, inverse):
    h = gram.shape[0] // 2
    g21 = gram[h:, :h] * scale
    w11 = inverse_factor(gram[:h, :h] * scale)
    l21 = dot_high(g21, w11, ((1,), (1,)))
    w22 = inverse_factor(gram[h:, h:] * scale - dot_high(l21, l21, ((1,), (1,))))
    inverse[:h, :h] = w11
    inverse[:h, h:] = jnp.zeros((h, h), jnp.float32)
    inverse[h:, :h] = -dot_high(w22, dot_high(l21, w11, ((1,), (0,))), ((1,), (0,)))
    inverse[h:, h:] = w22


def basis_kernel(scale, gram, product, basis, inverse):
    n = gram.shape[0]
    line = lax.broadcasted_iota(jnp.int32, (n, n), 0)
    lane = lax.broadcasted_iota(jnp.int32, (n, n), 1)
    one = (line == lane).astype(jnp.float32)
    weight = jnp.where(line > lane, 1.0, 0.5 * one)
    g = gram[...] * scale
    d_line = lax.rsqrt(jnp.sum(g * one, axis=1, keepdims=True))
    d_lane = lax.rsqrt(jnp.sum(g * one, axis=0, keepdims=True))
    w = (one - weight * (g * d_line * d_lane - one)) * d_lane
    for turn in range(2):
        off = dot_high(dot_high(w, g, ((1,), (0,))), w, ((1,), (1,))) - one
        w = w - dot_high(weight * off, w, ((1,), (0,)))
    inverse[...] = w
    settled = jnp.sum(off * off) < 1e-6

    @pl.when(jnp.logical_not(settled))
    def _():
        eliminated(gram, scale, inverse)

    basis[...] = dot_high(product[...], inverse[...], ((1,), (1,)))


def new_basis(gram, product, nodes):
    vmem = pl.BlockSpec(memory_space=pltpu.VMEM)
    return pl.pallas_call(
        functools.partial(basis_kernel, 1.0 / nodes),
        out_shape=jax.ShapeDtypeStruct(product.shape, jnp.float32),
        in_specs=[vmem, vmem],
        out_specs=vmem,
        scratch_shapes=[pltpu.VMEM(gram.shape, jnp.float32)],
        compiler_params=pltpu.CompilerParams(vmem_limit_bytes=VMEM_LIMIT),
        name="new_basis",
    )(gram, product)


def shards(panel, lists, tiles):
    nz, nx, ny, nc = axis_sizes()
    group = ny * nc
    plane = nx * group
    tile = tiles.shape[1]
    width = panel.shape[1]
    blocks = panel.shape[0] // tile
    nodes = panel.shape[0] * nz * plane
    his = nz // group
    own = panel.reshape(blocks, tile, width)
    entries = lists.reshape(3, his, group, nx).transpose(3, 2, 1, 0).reshape(plane, 1, 3 * his)
    entries = jnp.pad(entries.astype(jnp.float32), ((0, 0), (his, 7 - his), (0, 128 - 3 * his)))
    here, meta, cols, rows = bring(own, entries, tiles.reshape(his, group * nx, tile, tile))
    rows = rows.reshape(plane, blocks, tile, width)
    picks = meta[:, his, : 3 * his].astype(jnp.int32).reshape(plane * his, 3).T
    fwd, bwd = tile_products(picks, here, meta, cols, rows)
    product, gram = device_sums(
        fwd.reshape(plane, blocks * tile, width), bwd.reshape(his, group * blocks * tile, width)
    )
    return new_basis(gram, product, nodes)


def solution(mesh):
    sizes = mesh.devices.shape
    nx, ny, nc = grid_of(sizes)
    fine = Mesh(mesh.devices.reshape(sizes[0] // nx, nx, ny, nc), AXES)
    return jax.shard_map(
        shards,
        mesh=fine,
        in_specs=(P(AXES, None), P(None, AXES), P(AXES, None, None)),
        out_specs=P(AXES, None),
        check_vma=False,
    )


def grid_of(sizes):
    return (4, 4, 2) if sizes == (64, 8) else (2, 1, 2)
```

```python
import functools

import jax
import jax.numpy as jnp
from jax import lax
from jax.experimental import pallas as pl
from jax.experimental.pallas import tpu as pltpu
from jax.sharding import Mesh, PartitionSpec as P

HIGHEST = lax.Precision.HIGHEST
MESH = pl.DeviceIdType.MESH
VMEM_LIMIT = 56 * 1024 * 1024
AXES = ("z", "x", "y", "core")


def axis_sizes():
    return tuple(lax.axis_size(a) for a in AXES)


def split2(t):
    high = t.astype(jnp.bfloat16)
    low = (t - high.astype(jnp.float32)).astype(jnp.bfloat16)
    return high, low


CODE_TOP = 32767.0


def bring_kernel(
    sizes,
    panel,
    lists,
    tiles,
    here,
    meta,
    cols,
    rows,
    stage,
    coded,
    message,
    passing,
    local_sem,
    tile_sent,
    tile_came,
    list_sent,
    list_came,
    hold_sent,
    hold_came,
    ring_sent,
    ring_came,
    first_sent,
    first_came,
    second_sent,
    second_came,
    core_sent,
    core_came,
):
    nz, nx, ny, nc = sizes
    group = ny * nc
    plane = nx * group
    half = nz // 2
    z, x, y, c = (lax.axis_index(a) for a in AXES)
    g = y * nc + c
    me = x * group + g
    blocks = panel.shape[0]

    def member(p):
        return (z, x, p // nc, lax.rem(p, nc))

    def plane_peer(k):
        across = lax.rem(k, nx)
        px = lax.rem(x + across, nx)
        py = lax.rem(y + lax.rem(k // nx, ny) + across, ny)
        pc = lax.rem(c + k // (nx * ny), nc)
        return px * group + py * nc + pc, (z, px, py, pc)

    def remote(source, target, send_sem, recv_sem, device):
        return pltpu.make_async_remote_copy(
            src_ref=source,
            dst_ref=target,
            send_sem=send_sem,
            recv_sem=recv_sem,
            device_id=device,
            device_id_type=MESH,
        )

    above = (lax.rem(z + 1, nz), x, y, c)
    below = (lax.rem(z + nz - 1, nz), x, y, c)
    other = (z, x, y, nc - 1 - c)

    barrier = pltpu.get_barrier_semaphore()

    def greet(k, carry):
        pl.semaphore_signal(barrier, inc=1, device_id=plane_peer(k)[1], device_id_type=MESH)
        return carry

    lax.fori_loop(1, plane, greet, 0)
    for device in (above, below):
        pl.semaphore_signal(barrier, inc=1, device_id=device, device_id_type=MESH)

    local = [
        pltpu.make_async_copy(panel, rows.at[x, y, c], local_sem.at[0]),
        pltpu.make_async_copy(coded.at[me], here.at[me], local_sem.at[1]),
        pltpu.make_async_copy(message.at[me], meta.at[me], local_sem.at[2]),
    ]
    load = pltpu.make_async_copy(tiles, stage, local_sem.at[3])
    load.start()
    local[0].start()

    pl.semaphore_wait(barrier, plane - 1 + 2)

    def ring_copy(way, k, q, device):
        source = panel if k == 1 else passing.at[q]
        return remote(source, passing.at[q], ring_sent.at[way, k], ring_came.at[way, k], device)

    def to_holder(k, q, source, of):
        return remote(
            source,
            cols.at[q // group, pl.ds(of * blocks, blocks)],
            hold_sent.at[k],
            hold_came.at[q // group, of],
            member(lax.rem(q, group)),
        )

    def keep_block(k, q, source):
        return pltpu.make_async_copy(
            source, cols.at[q // group, pl.ds(g * blocks, blocks)], hold_sent.at[k]
        )

    def hand_over(k, q, source):
        @pl.when(lax.rem(q, group) == g)
        def _():
            keep_block(k, q, source).start()

        @pl.when(lax.rem(q, group) != g)
        def _():
            to_holder(k, q, source, g).start()

    def at_ring(k):
        return lax.rem(z + k + nz, nz)

    ring_copy(0, 1, z, above).start()
    ring_copy(1, 1, z, below).start()
    hand_over(0, z, panel)

    def ring_step(k):
        q = at_ring(-k)
        ring_copy(0, k, q, above).wait_recv()
        if k < half:
            ring_copy(0, k + 1, q, above).start()
        hand_over(2 * k - 1, q, passing.at[q])
        if k < half:
            q = at_ring(k)
            ring_copy(1, k, q, below).wait_recv()
            if k < half - 1:
                ring_copy(1, k + 1, q, below).start()
            hand_over(2 * k, q, passing.at[q])

    def first_x(k, p, at):
        return remote(
            panel.at[0], rows.at[at, y, c, 0], first_sent.at[0, k], first_came.at[0, at], (z, p, y, c)
        )

    def first_y(k, p, at):
        return remote(
            panel.at[1], rows.at[x, at, c, 1], first_sent.at[1, k], first_came.at[1, at], (z, x, p, c)
        )

    for k in range(1, nx):
        first_x(k, lax.rem(x + k, nx), x).start()
    for k in range(1, ny):
        first_y(k, lax.rem(y + k, ny), y).start()

    def tile_copy(k, p, device, at):
        return remote(coded.at[p], here.at[at], tile_sent.at[k], tile_came.at[at], device)

    def list_copy(k, p, device, at):
        return remote(message.at[p], meta.at[at], list_sent.at[k], list_came.at[at], device)

    def code(p):
        to = lax.rem(p, group) * nx + p // group
        entry = lists[p]
        for h in range(tiles.shape[0]):
            t = stage[h, to]
            top = jnp.maximum(jnp.max(jnp.abs(t), axis=0, keepdims=True), 1e-30)
            coded[p, h] = jnp.round(t * (CODE_TOP / top)).astype(jnp.int32).astype(jnp.int16)
            line = lax.broadcasted_iota(jnp.int32, entry.shape, 0)
            entry = jnp.where(line == h, top * (1.0 / CODE_TOP), entry)
        message[p] = entry

    def start_tiles(k, carry):
        p, device = plane_peer(k)
        code(p)
        list_copy(k, p, device, me).start()
        tile_copy(k, p, device, me).start()
        return carry

    load.wait()
    lax.fori_loop(1, plane, start_tiles, 0)
    code(me)
    local[1].start()
    local[2].start()

    cut = (1 + half // 4, 1 + (3 * half) // 4)
    for k in range(1, cut[0]):
        ring_step(k)

    def second_y(k, p, at):
        part = rows.at[:, at, c, 0]
        return remote(part, part, second_sent.at[0, k], second_came.at[0, at], (z, x, p, c))

    def second_x(k, p, at):
        part = rows.at[at, :, c, 1]
        return remote(part, part, second_sent.at[1, k], second_came.at[1, at], (z, p, y, c))

    for copy in local:
        copy.wait()
    for k in range(1, nx):
        p = lax.rem(x + k, nx)
        first_x(k, p, p).wait_recv()
    for k in range(1, ny):
        second_y(k, lax.rem(y + k, ny), y).start()
    for k in range(1, ny):
        p = lax.rem(y + k, ny)
        first_y(k, p, p).wait_recv()
    for k in range(1, nx):
        second_x(k, lax.rem(x + k, nx), x).start()

    for k in range(cut[0], cut[1]):
        ring_step(k)

    def core_y(p, of):
        part = rows.at[:, p, of, 0]
        return remote(part, part, core_sent.at[0, p], core_came.at[0, p], other)

    def core_x(p, of):
        part = rows.at[p, :, of, 1]
        return remote(part, part, core_sent.at[1, p], core_came.at[1, p], other)

    core_y(y, c).start()
    core_x(x, c).start()
    for k in range(1, ny):
        p = lax.rem(y + k, ny)
        second_y(k, p, p).wait_recv()
        core_y(p, c).start()
    for k in range(1, nx):
        p = lax.rem(x + k, nx)
        second_x(k, p, p).wait_recv()
        core_x(p, c).start()

    for k in range(cut[1], half + 1):
        ring_step(k)

    def finish(k, carry):
        p, device = plane_peer(k)
        tile_copy(k, p, device, p).wait_recv()
        list_copy(k, p, device, p).wait_recv()
        tile_copy(k, p, device, me).wait_send()
        list_copy(k, p, device, me).wait_send()
        return carry

    lax.fori_loop(1, plane, finish, 0)
    for p in range(ny):
        core_y(p, nc - 1 - c).wait_recv()
        core_y(p, c).wait_send()
    for p in range(nx):
        core_x(p, nc - 1 - c).wait_recv()
        core_x(p, c).wait_send()
    for k in range(1, nx):
        p = lax.rem(x + k, nx)
        first_x(k, p, x).wait_send()
        second_x(k, p, x).wait_send()
    for k in range(1, ny):
        p = lax.rem(y + k, ny)
        first_y(k, p, y).wait_send()
        second_y(k, p, y).wait_send()

    for k in range(1, half + 1):
        ring_copy(0, k, at_ring(1 - k), above).wait_send()
        if k < half:
            ring_copy(1, k, at_ring(k - 1), below).wait_send()
    for k in range(nz):
        q = z if k == 0 else at_ring(-(k + 1) // 2 if k % 2 else k // 2)
        source = panel if k == 0 else passing.at[q]

        @pl.when(lax.rem(q, group) == g)
        def _(k=k, q=q, source=source):
            keep_block(k, q, source).wait()

        @pl.when(lax.rem(q, group) != g)
        def _(k=k, q=q, source=source):
            to_holder(k, q, source, g).wait_send()

    for h in range(nz // group):
        for m in range(1, group):
            of = lax.rem(g + m, group)
            to_holder(0, h * group + g, panel, of).wait_recv()


def bring(panel, lists, tiles):
    sizes = axis_sizes()
    nz, nx, ny, nc = sizes
    group = ny * nc
    plane = nx * group
    blocks, tile, width = panel.shape
    his = nz // group
    span = group * blocks
    anywhere = pl.BlockSpec(memory_space=pl.ANY)
    dma = pltpu.SemaphoreType.DMA
    most = max(nx, ny)
    return pl.pallas_call(
        functools.partial(bring_kernel, sizes),
        out_shape=[
            jax.ShapeDtypeStruct((plane, his, tile, tile), jnp.int16),
            jax.ShapeDtypeStruct(lists.shape, jnp.float32),
            jax.ShapeDtypeStruct((his, span, tile, width), jnp.bfloat16),
            jax.ShapeDtypeStruct((nx, ny, nc, blocks, tile, width), jnp.bfloat16),
        ],
        in_specs=[anywhere, pl.BlockSpec(memory_space=pltpu.VMEM), anywhere],
        out_specs=[anywhere] * 4,
        scratch_shapes=[
            pltpu.VMEM(tiles.shape, jnp.float32),
            pltpu.VMEM((plane, his, tile, tile), jnp.int16),
            pltpu.VMEM(lists.shape, jnp.float32),
            pltpu.VMEM((nz, blocks, tile, width), jnp.bfloat16),
            dma((4,)),
            dma((plane,)),
            dma((plane,)),
            dma((plane,)),
            dma((plane,)),
            dma((nz,)),
            dma((his, group)),
            dma((2, nz // 2 + 1)),
            dma((2, nz // 2 + 1)),
            dma((2, most)),
            dma((2, most)),
            dma((2, most)),
            dma((2, most)),
            dma((2, most)),
            dma((2, most)),
        ],
        compiler_params=pltpu.CompilerParams(
            collective_id=1, has_side_effects=True, vmem_limit_bytes=VMEM_LIMIT
        ),
        name="bring",
    )(panel, lists, tiles)


def tiles_kernel(his, blocks, span, step, meta, tiles, scales, cols, rows, fwd, bwd):
    at = pl.program_id(0)

    @pl.when(at == 0)
    def _():
        bwd[...] = jnp.zeros_like(bwd)

    for u in range(step):
        src = at * step + u
        values, panels, picks = [], [], []
        for hi in range(his):
            slot = src * his + hi
            row, col, live = meta[0, slot], meta[1, slot], meta[2, slot]
            scale = scales[u, hi : hi + 1] * live.astype(jnp.float32)
            t = tiles[u, hi].astype(jnp.int32).astype(jnp.float32) * scale
            values.append(t)
            picks.append(row)
            panels.append(cols[hi, col])
            flipped = jnp.concatenate(split2(t.T), axis=1)
            own = rows[u, row]
            got = jnp.dot(
                flipped, jnp.concatenate([own, own], axis=0), preferred_element_type=jnp.float32
            )
            bwd[hi, col] += got
        left = jnp.concatenate(
            [
                jnp.concatenate(
                    [t * (pick == b).astype(jnp.float32) for t, pick in zip(values, picks)], axis=1
                )
                for b in range(blocks)
            ],
            axis=0,
        )
        right = jnp.concatenate(panels, axis=0)
        high, low = split2(left)
        out = jnp.dot(high, right, preferred_element_type=jnp.float32) + jnp.dot(
            low, right, preferred_element_type=jnp.float32
        )
        fwd[u] = out.reshape(fwd.shape[1:])


def tile_products(meta, tiles, scales, cols, rows):
    plane, his, tile, _ = tiles.shape
    blocks, width = rows.shape[1], rows.shape[3]
    span = cols.shape[1]
    step = 4
    return pl.pallas_call(
        functools.partial(tiles_kernel, his, blocks, span, step),
        grid_spec=pltpu.PrefetchScalarGridSpec(
            num_scalar_prefetch=1,
            grid=(plane // step,),
            in_specs=[
                pl.BlockSpec((step, his, tile, tile), lambda i, m: (i, 0, 0, 0)),
                pl.BlockSpec((step,) + scales.shape[1:], lambda i, m: (i, 0, 0)),
                pl.BlockSpec(cols.shape, lambda i, m: (0, 0, 0, 0)),
                pl.BlockSpec((step, blocks, tile, width), lambda i, m: (i, 0, 0, 0)),
            ],
            out_specs=[
                pl.BlockSpec((step, blocks, tile, width), lambda i, m: (i, 0, 0, 0)),
                pl.BlockSpec((his, span, tile, width), lambda i, m: (0, 0, 0, 0)),
            ],
        ),
        out_shape=[
            jax.ShapeDtypeStruct((plane, blocks, tile, width), jnp.float32),
            jax.ShapeDtypeStruct((his, span, tile, width), jnp.float32),
        ],
        compiler_params=pltpu.CompilerParams(vmem_limit_bytes=VMEM_LIMIT),
        name="tile_products",
    )(meta, tiles, scales, cols, rows)


CHUNK = 64
SKEW = 3


def sums_kernel(
    sizes,
    fwd,
    bwd,
    product,
    gram,
    held,
    keep,
    from_core,
    from_x,
    from_y,
    end_x,
    end_y,
    from_below,
    from_above,
    last,
    part,
    got,
    ring,
    whole,
    local_sem,
    chain_sent,
    chain_came,
    last_sent,
    last_came,
    plane_sent,
    plane_came,
    sent,
    came,
):
    nz, nx, ny, nc = sizes
    group = ny * nc
    plane = nx * group
    half = nz // 2
    z, x, y, c = (lax.axis_index(a) for a in AXES)
    g = y * nc + c
    me = x * group + g
    strip = part.shape[0] // plane
    chunks = held.shape[1]
    per_device = last.shape[0]

    def member(p):
        return (z, x, p // nc, lax.rem(p, nc))

    def plane_peer(k):
        p = lax.rem(me + k, plane)
        return p, (z, p // group, lax.rem(p, group) // nc, lax.rem(p, nc))

    def ring_peer(k):
        q = lax.rem(z + k, nz)
        return q, (q, x, y, c)

    def remote(source, target, send_sem, recv_sem, device):
        return pltpu.make_async_remote_copy(
            src_ref=source,
            dst_ref=target,
            send_sem=send_sem,
            recv_sem=recv_sem,
            device_id=device,
            device_id_type=MESH,
        )

    barrier = pltpu.get_barrier_semaphore()

    def greet(peer):
        def body(k, carry):
            pl.semaphore_signal(barrier, inc=1, device_id=peer(k)[1], device_id_type=MESH)
            return carry

        return body

    lax.fori_loop(1, plane, greet(plane_peer), 0)
    lax.fori_loop(1, nz, greet(ring_peer), 0)
    load_held = pltpu.make_async_copy(bwd, held, local_sem.at[0])
    load_keep = pltpu.make_async_copy(fwd.at[:, :, c], keep, local_sem.at[1])
    load_held.start()
    load_keep.start()
    pl.semaphore_wait(barrier, plane - 1 + nz - 1)

    other = (z, x, y, nc - 1 - c)
    core_copy = remote(
        fwd.at[:, :, nc - 1 - c], from_core, plane_sent.at[0, 0], plane_came.at[0, 0], other
    )
    core_copy.start()

    d0 = lax.rem(g - z + nz, nz)
    lower = jnp.logical_and(d0 >= 1, d0 <= half)
    hu = jnp.where(lower, 0, 1)
    hd = 1 - hu
    du = jnp.where(lower, d0, lax.rem(d0 + half, nz))
    pu = half - du
    pd = du - 1
    target = du == half
    above = (lax.rem(z + 1, nz), x, y, c)
    below = (lax.rem(z + nz - 1, nz), x, y, c)

    def up(j):
        return remote(
            held.at[hu, j], from_below.at[j], chain_sent.at[0, j], chain_came.at[0, j], above
        )

    def down(j):
        return remote(
            held.at[hd, j], from_above.at[j], chain_sent.at[1, j], chain_came.at[1, j], below
        )

    def scatter(j, at):
        return remote(
            held.at[hd, j], last.at[at], last_sent.at[j], last_came.at[at], member(j // per_device)
        )

    load_held.wait()

    def step(i, carry):
        j = i - SKEW * pu

        @pl.when(jnp.logical_and(j >= 0, j < chunks))
        def _():
            @pl.when(pu > 0)
            def _():
                up(j).wait_recv()
                held[hu, j] += from_below[j]

            up(j).start()

        jd = i - SKEW * pd

        @pl.when(jnp.logical_and(jnp.logical_not(target), jnp.logical_and(jd >= 0, jd < chunks)))
        def _():
            @pl.when(pd > 0)
            def _():
                down(jd).wait_recv()
                held[hd, jd] += from_above[jd]

            down(jd).start()

        jt = i - SKEW * half

        @pl.when(jnp.logical_and(target, jnp.logical_and(jt >= 0, jt < chunks)))
        def _():
            up(jt).wait_recv()
            down(jt).wait_recv()
            held[hd, jt] += from_below[jt] + from_above[jt]
            at = lax.rem(jt, per_device)

            @pl.when(jt // per_device == g)
            def _():
                last[at] = held[hd, jt]

            @pl.when(jt // per_device != g)
            def _():
                scatter(jt, at).start()

        return carry

    steps = chunks + SKEW * half
    cut = (steps // 6, (3 * steps) // 5)
    lax.fori_loop(0, cut[0], step, 0)

    load_keep.wait()
    core_copy.wait()
    rows = keep.shape[2]
    top, low = pl.ds(0, rows // 2), pl.ds(rows // 2, rows // 2)

    def add_core(i, carry):
        at = (i // ny, lax.rem(i, ny))
        keep[at] += from_core[at]
        return carry

    lax.fori_loop(0, nx * ny, add_core, 0)

    def x_copy(k):
        p = lax.rem(x + k, nx)
        return remote(
            keep.at[p, :, top],
            from_x.at[x],
            plane_sent.at[1, k],
            plane_came.at[1, x],
            (z, p, y, c),
        )

    def y_copy(k):
        p = lax.rem(y + k, ny)
        return remote(
            keep.at[:, p, low],
            from_y.at[y],
            plane_sent.at[2, k],
            plane_came.at[2, y],
            (z, x, p, c),
        )

    for k in range(1, max(nx, ny)):
        if k < nx:
            x_copy(k).start()
        if k < ny:
            y_copy(k).start()

    lax.fori_loop(cut[0], cut[1], step, 0)

    def x_source(k):
        p = lax.rem(x + k, nx)
        return p, remote(
            from_x.at[p], from_x.at[p], plane_sent.at[1, k], plane_came.at[1, p], (z, p, y, c)
        )

    def y_source(k):
        p = lax.rem(y + k, ny)
        return p, remote(
            from_y.at[p], from_y.at[p], plane_sent.at[2, k], plane_came.at[2, p], (z, x, p, c)
        )

    for k in range(1, nx):
        p, copy = x_source(k)
        copy.wait_recv()
        keep[x, :, top] += from_x[p]
    for k in range(1, ny):
        p, copy = y_source(k)
        copy.wait_recv()
        keep[:, y, low] += from_y[p]

    def last_y(k, at):
        p = lax.rem(y + k, ny)
        return remote(
            keep.at[x, p, top],
            end_y.at[at],
            plane_sent.at[3, k],
            plane_came.at[3, at],
            (z, x, p, c),
        )

    def last_x(k, at):
        p = lax.rem(x + k, nx)
        return remote(
            keep.at[p, y, low],
            end_x.at[at],
            plane_sent.at[4, k],
            plane_came.at[4, at],
            (z, p, y, c),
        )

    for k in range(1, max(nx, ny)):
        if k < ny:
            last_y(k, y).start()
        if k < nx:
            last_x(k, x).start()

    lax.fori_loop(cut[1], steps, step, 0)

    upper = keep[x, y, top]
    for k in range(1, ny):
        p = lax.rem(y + k, ny)
        last_y(k, p).wait_recv()
        upper = upper + end_y[p]
    lower_rows = keep[x, y, low]
    for k in range(1, nx):
        p = lax.rem(x + k, nx)
        last_x(k, p).wait_recv()
        lower_rows = lower_rows + end_x[p]
    total = jnp.concatenate([upper, lower_rows], axis=0)
    holder = lax.rem(z, group)

    @pl.when(holder != g)
    def _():
        for at in range(per_device):
            scatter(at, at).wait_recv()

    total = total + last[...].reshape(total.shape)
    product[...] = total
    part[...] = lax.dot_general(
        total, total, (((0,), (0,)), ((), ())), precision=HIGHEST, preferred_element_type=jnp.float32
    )

    def rows_of(p):
        return pl.ds(pl.multiple_of(p * strip, strip), strip)

    def exchange(count, peer, stage, mine, source, target_of):
        def copy(k, p, device):
            return remote(
                source(p), target_of(mine), sent.at[stage, k], came.at[stage, mine], device
            )

        def start(k, carry):
            p, device = peer(k)
            copy(k, p, device).start()
            return carry

        def finish(k, carry):
            p, device = peer(k)
            copy(k, p, device).wait_send()
            remote(
                target_of(p), target_of(p), sent.at[stage, k], came.at[stage, p], device
            ).wait_recv()
            return carry

        lax.fori_loop(1, count, start, 0)
        lax.fori_loop(1, count, finish, 0)

    exchange(plane, plane_peer, 0, me, lambda p: part.at[rows_of(p)], lambda p: got.at[p])
    strip_sum = part[rows_of(me)]
    for k in range(1, plane):
        strip_sum = strip_sum + got[lax.rem(me + k, plane)]
    ring[z] = strip_sum
    exchange(nz, ring_peer, 1, z, lambda p: ring.at[z], lambda p: ring.at[p])
    strip_sum = ring[0]
    for k in range(1, nz):
        strip_sum = strip_sum + ring[k]
    whole[rows_of(me)] = strip_sum
    exchange(
        plane, plane_peer, 2, me, lambda p: whole.at[rows_of(me)], lambda p: whole.at[rows_of(p)]
    )
    gram[...] = whole[...]

    for k in range(1, nx):
        x_copy(k).wait_send()
        last_x(k, x).wait_send()
    for k in range(1, ny):
        y_copy(k).wait_send()
        last_y(k, y).wait_send()

    def drain(j, carry):
        up(j).wait_send()

        @pl.when(jnp.logical_not(target))
        def _():
            down(j).wait_send()

        @pl.when(jnp.logical_and(target, j // per_device != g))
        def _():
            scatter(j, lax.rem(j, per_device)).wait_send()

        return carry

    lax.fori_loop(0, chunks, drain, 0)


def device_sums(fwd, bwd):
    sizes = axis_sizes()
    nz, nx, ny, nc = sizes
    group = ny * nc
    plane = nx * group
    _, rows, width = fwd.shape
    strip = width // plane
    most = max(plane, nz)
    chunks = group * rows // CHUNK
    fwd = fwd.reshape(nx, ny, nc, rows, width)
    bwd = bwd.reshape(2, chunks, CHUNK, width)
    vmem = pl.BlockSpec(memory_space=pltpu.VMEM)
    anywhere = pl.BlockSpec(memory_space=pl.ANY)

    def buffer(*shape):
        return pltpu.VMEM(shape, jnp.float32)

    dma = pltpu.SemaphoreType.DMA
    return pl.pallas_call(
        functools.partial(sums_kernel, sizes),
        out_shape=[
            jax.ShapeDtypeStruct((rows, width), jnp.float32),
            jax.ShapeDtypeStruct((width, width), jnp.float32),
        ],
        in_specs=[anywhere, anywhere],
        out_specs=[vmem, vmem],
        scratch_shapes=[
            buffer(2, chunks, CHUNK, width),
            buffer(nx, ny, rows, width),
            buffer(nx, ny, rows, width),
            buffer(nx, ny, rows // 2, width),
            buffer(ny, nx, rows // 2, width),
            buffer(nx, rows // 2, width),
            buffer(ny, rows // 2, width),
            buffer(chunks, CHUNK, width),
            buffer(chunks, CHUNK, width),
            buffer(rows // CHUNK, CHUNK, width),
            buffer(width, width),
            buffer(plane, strip, width),
            buffer(nz, strip, width),
            buffer(width, width),
            dma((2,)),
            dma((2, chunks)),
            dma((2, chunks)),
            dma((chunks,)),
            dma((rows // CHUNK,)),
            dma((5, max(nx, ny))),
            dma((5, max(nx, ny))),
            dma((3, most)),
            dma((3, most)),
        ],
        compiler_params=pltpu.CompilerParams(
            collective_id=0, has_side_effects=True, vmem_limit_bytes=VMEM_LIMIT
        ),
        name="device_sums",
    )(fwd, bwd)


def dot_high(a, b, dims):
    return lax.dot_general(
        a, b, (dims, ((), ())), precision=HIGHEST, preferred_element_type=jnp.float32
    )


def inverse_factor(a):
    n = a.shape[0]
    sub = 8
    lanes = lax.broadcasted_iota(jnp.int32, (sub, n), 1)
    subs = lax.broadcasted_iota(jnp.int32, (sub, n), 0)
    left = [a[i * sub : (i + 1) * sub] for i in range(n // sub)]
    right = [(lanes == subs + i * sub).astype(jnp.float32) for i in range(n // sub)]
    for j in range(n):
        t0, s = divmod(j, sub)
        row = left[t0][s : s + 1]
        inv = 1.0 / row[:, j : j + 1]
        wrow = right[t0][s : s + 1]
        scaled = row * inv
        wscaled = wrow * inv
        for t in range(t0, n // sub):
            col = left[t][:, j : j + 1]
            if t == t0:
                col = jnp.where(subs[:, :1] > s, col, 0.0)
            left[t] = left[t] - col * scaled
            right[t] = right[t] - col * wscaled
    out = []
    for t in range(n // sub):
        d = jnp.sum(jnp.where(lanes == subs + t * sub, left[t], 0.0), axis=1, keepdims=True)
        out.append(right[t] * lax.rsqrt(d))
    return jnp.concatenate(out, axis=0)


def eliminated(gram, scale, inverse):
    h = gram.shape[0] // 2
    g21 = gram[h:, :h] * scale
    w11 = inverse_factor(gram[:h, :h] * scale)
    l21 = dot_high(g21, w11, ((1,), (1,)))
    w22 = inverse_factor(gram[h:, h:] * scale - dot_high(l21, l21, ((1,), (1,))))
    inverse[:h, :h] = w11
    inverse[:h, h:] = jnp.zeros((h, h), jnp.float32)
    inverse[h:, :h] = -dot_high(w22, dot_high(l21, w11, ((1,), (0,))), ((1,), (0,)))
    inverse[h:, h:] = w22


def basis_kernel(scale, gram, product, basis, inverse):
    n = gram.shape[0]
    line = lax.broadcasted_iota(jnp.int32, (n, n), 0)
    lane = lax.broadcasted_iota(jnp.int32, (n, n), 1)
    one = (line == lane).astype(jnp.float32)
    weight = jnp.where(line > lane, 1.0, 0.5 * one)
    g = gram[...] * scale
    d_line = lax.rsqrt(jnp.sum(g * one, axis=1, keepdims=True))
    d_lane = lax.rsqrt(jnp.sum(g * one, axis=0, keepdims=True))
    w = (one - weight * (g * d_line * d_lane - one)) * d_lane
    for turn in range(2):
        off = dot_high(dot_high(w, g, ((1,), (0,))), w, ((1,), (1,))) - one
        w = w - dot_high(weight * off, w, ((1,), (0,)))
    inverse[...] = w
    settled = jnp.sum(off * off) < 1e-6

    @pl.when(jnp.logical_not(settled))
    def _():
        eliminated(gram, scale, inverse)

    basis[...] = dot_high(product[...], inverse[...], ((1,), (1,)))


def new_basis(gram, product, nodes):
    vmem = pl.BlockSpec(memory_space=pltpu.VMEM)
    return pl.pallas_call(
        functools.partial(basis_kernel, 1.0 / nodes),
        out_shape=jax.ShapeDtypeStruct(product.shape, jnp.float32),
        in_specs=[vmem, vmem],
        out_specs=vmem,
        scratch_shapes=[pltpu.VMEM(gram.shape, jnp.float32)],
        compiler_params=pltpu.CompilerParams(vmem_limit_bytes=VMEM_LIMIT),
        name="new_basis",
    )(gram, product)


def shards(panel, lists, tiles):
    nz, nx, ny, nc = axis_sizes()
    group = ny * nc
    plane = nx * group
    tile = tiles.shape[1]
    width = panel.shape[1]
    blocks = panel.shape[0] // tile
    nodes = panel.shape[0] * nz * plane
    his = nz // group
    own = panel.reshape(blocks, tile, width)
    entries = lists.reshape(3, his, group, nx).transpose(3, 2, 1, 0).reshape(plane, 1, 3 * his)
    entries = jnp.pad(entries.astype(jnp.float32), ((0, 0), (his, 7 - his), (0, 128 - 3 * his)))
    here, meta, cols, rows = bring(own, entries, tiles.reshape(his, group * nx, tile, tile))
    rows = rows.reshape(plane, blocks, tile, width)
    picks = meta[:, his, : 3 * his].astype(jnp.int32).reshape(plane * his, 3).T
    fwd, bwd = tile_products(picks, here, meta, cols, rows)
    product, gram = device_sums(
        fwd.reshape(plane, blocks * tile, width), bwd.reshape(his, group * blocks * tile, width)
    )
    return new_basis(gram, product, nodes)


def solution(mesh):
    sizes = mesh.devices.shape
    nx, ny, nc = grid_of(sizes)
    fine = Mesh(mesh.devices.reshape(sizes[0] // nx, nx, ny, nc), AXES)
    return jax.shard_map(
        shards,
        mesh=fine,
        in_specs=(P(AXES, None), P(None, AXES), P(AXES, None, None)),
        out_specs=P(AXES, None),
        check_vma=False,
    )


def grid_of(sizes):
    return (4, 4, 2) if sizes == (64, 8) else (2, 1, 2)
```

```python
import functools

import jax
import jax.numpy as jnp
from jax import lax
from jax.experimental import pallas as pl
from jax.experimental.pallas import tpu as pltpu
from jax.sharding import Mesh, PartitionSpec as P

HIGHEST = lax.Precision.HIGHEST
MESH = pl.DeviceIdType.MESH
VMEM_LIMIT = 56 * 1024 * 1024
AXES = ("z", "x", "y", "core")


def axis_sizes():
    return tuple(lax.axis_size(a) for a in AXES)


def split2(t):
    high = t.astype(jnp.bfloat16)
    low = (t - high.astype(jnp.float32)).astype(jnp.bfloat16)
    return high, low


CODE_TOP = 32767.0


def bring_kernel(
    sizes,
    panel,
    lists,
    tiles,
    here,
    meta,
    cols,
    rows,
    stage,
    coded,
    message,
    passing,
    local_sem,
    tile_sent,
    tile_came,
    list_sent,
    list_came,
    hold_sent,
    hold_came,
    ring_sent,
    ring_came,
    first_sent,
    first_came,
    second_sent,
    second_came,
    core_sent,
    core_came,
):
    nz, nx, ny, nc = sizes
    group = ny * nc
    plane = nx * group
    half = nz // 2
    z, x, y, c = (lax.axis_index(a) for a in AXES)
    g = y * nc + c
    me = x * group + g
    blocks = panel.shape[0]

    def member(p):
        return (z, x, p // nc, lax.rem(p, nc))

    def plane_peer(k):
        across = lax.rem(k, nx)
        px = lax.rem(x + across, nx)
        py = lax.rem(y + lax.rem(k // nx, ny) + across, ny)
        pc = lax.rem(c + k // (nx * ny), nc)
        return px * group + py * nc + pc, (z, px, py, pc)

    def remote(source, target, send_sem, recv_sem, device):
        return pltpu.make_async_remote_copy(
            src_ref=source,
            dst_ref=target,
            send_sem=send_sem,
            recv_sem=recv_sem,
            device_id=device,
            device_id_type=MESH,
        )

    above = (lax.rem(z + 1, nz), x, y, c)
    below = (lax.rem(z + nz - 1, nz), x, y, c)
    other = (z, x, y, nc - 1 - c)

    barrier = pltpu.get_barrier_semaphore()

    def greet(k, carry):
        pl.semaphore_signal(barrier, inc=1, device_id=plane_peer(k)[1], device_id_type=MESH)
        return carry

    lax.fori_loop(1, plane, greet, 0)
    for device in (above, below):
        pl.semaphore_signal(barrier, inc=1, device_id=device, device_id_type=MESH)

    local = [
        pltpu.make_async_copy(panel, rows.at[x, y, c], local_sem.at[0]),
        pltpu.make_async_copy(coded.at[me], here.at[me], local_sem.at[1]),
        pltpu.make_async_copy(message.at[me], meta.at[me], local_sem.at[2]),
    ]
    load = pltpu.make_async_copy(tiles, stage, local_sem.at[3])
    load.start()
    local[0].start()

    pl.semaphore_wait(barrier, plane - 1 + 2)

    def ring_copy(way, k, q, device):
        source = panel if k == 1 else passing.at[q]
        return remote(source, passing.at[q], ring_sent.at[way, k], ring_came.at[way, k], device)

    def to_holder(k, q, source, of):
        return remote(
            source,
            cols.at[q // group, pl.ds(of * blocks, blocks)],
            hold_sent.at[k],
            hold_came.at[q // group, of],
            member(lax.rem(q, group)),
        )

    def keep_block(k, q, source):
        return pltpu.make_async_copy(
            source, cols.at[q // group, pl.ds(g * blocks, blocks)], hold_sent.at[k]
        )

    def hand_over(k, q, source):
        @pl.when(lax.rem(q, group) == g)
        def _():
            keep_block(k, q, source).start()

        @pl.when(lax.rem(q, group) != g)
        def _():
            to_holder(k, q, source, g).start()

    def at_ring(k):
        return lax.rem(z + k + nz, nz)

    ring_copy(0, 1, z, above).start()
    ring_copy(1, 1, z, below).start()
    hand_over(0, z, panel)

    def ring_step(k):
        q = at_ring(-k)
        ring_copy(0, k, q, above).wait_recv()
        if k < half:
            ring_copy(0, k + 1, q, above).start()
        hand_over(2 * k - 1, q, passing.at[q])
        if k < half:
            q = at_ring(k)
            ring_copy(1, k, q, below).wait_recv()
            if k < half - 1:
                ring_copy(1, k + 1, q, below).start()
            hand_over(2 * k, q, passing.at[q])

    def first_x(k, p, at):
        return remote(
            panel.at[0], rows.at[at, y, c, 0], first_sent.at[0, k], first_came.at[0, at], (z, p, y, c)
        )

    def first_y(k, p, at):
        return remote(
            panel.at[1], rows.at[x, at, c, 1], first_sent.at[1, k], first_came.at[1, at], (z, x, p, c)
        )

    for k in range(1, nx):
        first_x(k, lax.rem(x + k, nx), x).start()
    for k in range(1, ny):
        first_y(k, lax.rem(y + k, ny), y).start()

    def tile_copy(k, p, device, at):
        return remote(coded.at[p], here.at[at], tile_sent.at[k], tile_came.at[at], device)

    def list_copy(k, p, device, at):
        return remote(message.at[p], meta.at[at], list_sent.at[k], list_came.at[at], device)

    def code(p):
        to = lax.rem(p, group) * nx + p // group
        entry = lists[p]
        for h in range(tiles.shape[0]):
            t = stage[h, to]
            top = jnp.maximum(jnp.max(jnp.abs(t), axis=0, keepdims=True), 1e-30)
            coded[p, h] = jnp.round(t * (CODE_TOP / top)).astype(jnp.int32).astype(jnp.int16)
            line = lax.broadcasted_iota(jnp.int32, entry.shape, 0)
            entry = jnp.where(line == h, top * (1.0 / CODE_TOP), entry)
        message[p] = entry

    def start_tiles(k, carry):
        p, device = plane_peer(k)
        code(p)
        list_copy(k, p, device, me).start()
        tile_copy(k, p, device, me).start()
        return carry

    load.wait()
    lax.fori_loop(1, plane, start_tiles, 0)
    code(me)
    local[1].start()
    local[2].start()

    cut = (1 + half // 4, 1 + (3 * half) // 4)
    for k in range(1, cut[0]):
        ring_step(k)

    def second_y(k, p, at):
        part = rows.at[:, at, c, 0]
        return remote(part, part, second_sent.at[0, k], second_came.at[0, at], (z, x, p, c))

    def second_x(k, p, at):
        part = rows.at[at, :, c, 1]
        return remote(part, part, second_sent.at[1, k], second_came.at[1, at], (z, p, y, c))

    for copy in local:
        copy.wait()
    for k in range(1, nx):
        p = lax.rem(x + k, nx)
        first_x(k, p, p).wait_recv()
    for k in range(1, ny):
        second_y(k, lax.rem(y + k, ny), y).start()
    for k in range(1, ny):
        p = lax.rem(y + k, ny)
        first_y(k, p, p).wait_recv()
    for k in range(1, nx):
        second_x(k, lax.rem(x + k, nx), x).start()

    for k in range(cut[0], cut[1]):
        ring_step(k)

    def core_y(p, of):
        part = rows.at[:, p, of, 0]
        return remote(part, part, core_sent.at[0, p], core_came.at[0, p], other)

    def core_x(p, of):
        part = rows.at[p, :, of, 1]
        return remote(part, part, core_sent.at[1, p], core_came.at[1, p], other)

    core_y(y, c).start()
    core_x(x, c).start()
    for k in range(1, ny):
        p = lax.rem(y + k, ny)
        second_y(k, p, p).wait_recv()
        core_y(p, c).start()
    for k in range(1, nx):
        p = lax.rem(x + k, nx)
        second_x(k, p, p).wait_recv()
        core_x(p, c).start()

    for k in range(cut[1], half + 1):
        ring_step(k)

    def finish(k, carry):
        p, device = plane_peer(k)
        tile_copy(k, p, device, p).wait_recv()
        list_copy(k, p, device, p).wait_recv()
        tile_copy(k, p, device, me).wait_send()
        list_copy(k, p, device, me).wait_send()
        return carry

    lax.fori_loop(1, plane, finish, 0)
    for p in range(ny):
        core_y(p, nc - 1 - c).wait_recv()
        core_y(p, c).wait_send()
    for p in range(nx):
        core_x(p, nc - 1 - c).wait_recv()
        core_x(p, c).wait_send()
    for k in range(1, nx):
        p = lax.rem(x + k, nx)
        first_x(k, p, x).wait_send()
        second_x(k, p, x).wait_send()
    for k in range(1, ny):
        p = lax.rem(y + k, ny)
        first_y(k, p, y).wait_send()
        second_y(k, p, y).wait_send()

    for k in range(1, half + 1):
        ring_copy(0, k, at_ring(1 - k), above).wait_send()
        if k < half:
            ring_copy(1, k, at_ring(k - 1), below).wait_send()
    for k in range(nz):
        q = z if k == 0 else at_ring(-(k + 1) // 2 if k % 2 else k // 2)
        source = panel if k == 0 else passing.at[q]

        @pl.when(lax.rem(q, group) == g)
        def _(k=k, q=q, source=source):
            keep_block(k, q, source).wait()

        @pl.when(lax.rem(q, group) != g)
        def _(k=k, q=q, source=source):
            to_holder(k, q, source, g).wait_send()

    for h in range(nz // group):
        for m in range(1, group):
            of = lax.rem(g + m, group)
            to_holder(0, h * group + g, panel, of).wait_recv()


def bring(panel, lists, tiles):
    sizes = axis_sizes()
    nz, nx, ny, nc = sizes
    group = ny * nc
    plane = nx * group
    blocks, tile, width = panel.shape
    his = nz // group
    span = group * blocks
    anywhere = pl.BlockSpec(memory_space=pl.ANY)
    dma = pltpu.SemaphoreType.DMA
    most = max(nx, ny)
    return pl.pallas_call(
        functools.partial(bring_kernel, sizes),
        out_shape=[
            jax.ShapeDtypeStruct((plane, his, tile, tile), jnp.int16),
            jax.ShapeDtypeStruct(lists.shape, jnp.float32),
            jax.ShapeDtypeStruct((his, span, tile, width), jnp.bfloat16),
            jax.ShapeDtypeStruct((nx, ny, nc, blocks, tile, width), jnp.bfloat16),
        ],
        in_specs=[anywhere, pl.BlockSpec(memory_space=pltpu.VMEM), anywhere],
        out_specs=[anywhere] * 4,
        scratch_shapes=[
            pltpu.VMEM(tiles.shape, jnp.float32),
            pltpu.VMEM((plane, his, tile, tile), jnp.int16),
            pltpu.VMEM(lists.shape, jnp.float32),
            pltpu.VMEM((nz, blocks, tile, width), jnp.bfloat16),
            dma((4,)),
            dma((plane,)),
            dma((plane,)),
            dma((plane,)),
            dma((plane,)),
            dma((nz,)),
            dma((his, group)),
            dma((2, nz // 2 + 1)),
            dma((2, nz // 2 + 1)),
            dma((2, most)),
            dma((2, most)),
            dma((2, most)),
            dma((2, most)),
            dma((2, most)),
            dma((2, most)),
        ],
        compiler_params=pltpu.CompilerParams(
            collective_id=1, has_side_effects=True, vmem_limit_bytes=VMEM_LIMIT
        ),
        name="bring",
    )(panel, lists, tiles)


def tiles_kernel(his, blocks, span, step, meta, tiles, scales, cols, rows, fwd, bwd):
    at = pl.program_id(0)

    @pl.when(at == 0)
    def _():
        bwd[...] = jnp.zeros_like(bwd)

    for u in range(step):
        src = at * step + u
        values, panels, picks = [], [], []
        for hi in range(his):
            slot = src * his + hi
            row, col, live = meta[0, slot], meta[1, slot], meta[2, slot]
            scale = scales[u, hi : hi + 1] * live.astype(jnp.float32)
            t = tiles[u, hi].astype(jnp.int32).astype(jnp.float32) * scale
            values.append(t)
            picks.append(row)
            panels.append(cols[hi, col])
            flipped = jnp.concatenate(split2(t.T), axis=1)
            own = rows[u, row]
            got = jnp.dot(
                flipped, jnp.concatenate([own, own], axis=0), preferred_element_type=jnp.float32
            )
            bwd[hi, col] += got
        left = jnp.concatenate(
            [
                jnp.concatenate(
                    [t * (pick == b).astype(jnp.float32) for t, pick in zip(values, picks)], axis=1
                )
                for b in range(blocks)
            ],
            axis=0,
        )
        right = jnp.concatenate(panels, axis=0)
        high, low = split2(left)
        both = jnp.dot(
            jnp.concatenate([high, low], axis=0), right, preferred_element_type=jnp.float32
        )
        out = both[: left.shape[0]] + both[left.shape[0] :]
        fwd[u] = out.reshape(fwd.shape[1:])


def tile_products(meta, tiles, scales, cols, rows):
    plane, his, tile, _ = tiles.shape
    blocks, width = rows.shape[1], rows.shape[3]
    span = cols.shape[1]
    step = 4
    return pl.pallas_call(
        functools.partial(tiles_kernel, his, blocks, span, step),
        grid_spec=pltpu.PrefetchScalarGridSpec(
            num_scalar_prefetch=1,
            grid=(plane // step,),
            in_specs=[
                pl.BlockSpec((step, his, tile, tile), lambda i, m: (i, 0, 0, 0)),
                pl.BlockSpec((step,) + scales.shape[1:], lambda i, m: (i, 0, 0)),
                pl.BlockSpec(cols.shape, lambda i, m: (0, 0, 0, 0)),
                pl.BlockSpec((step, blocks, tile, width), lambda i, m: (i, 0, 0, 0)),
            ],
            out_specs=[
                pl.BlockSpec((step, blocks, tile, width), lambda i, m: (i, 0, 0, 0)),
                pl.BlockSpec((his, span, tile, width), lambda i, m: (0, 0, 0, 0)),
            ],
        ),
        out_shape=[
            jax.ShapeDtypeStruct((plane, blocks, tile, width), jnp.float32),
            jax.ShapeDtypeStruct((his, span, tile, width), jnp.float32),
        ],
        compiler_params=pltpu.CompilerParams(vmem_limit_bytes=VMEM_LIMIT),
        name="tile_products",
    )(meta, tiles, scales, cols, rows)


CHUNK = 64
SKEW = 3


def sums_kernel(
    sizes,
    fwd,
    bwd,
    product,
    gram,
    held,
    keep,
    from_core,
    from_x,
    from_y,
    end_x,
    end_y,
    from_below,
    from_above,
    last,
    part,
    got,
    ring,
    whole,
    local_sem,
    chain_sent,
    chain_came,
    last_sent,
    last_came,
    plane_sent,
    plane_came,
    sent,
    came,
):
    nz, nx, ny, nc = sizes
    group = ny * nc
    plane = nx * group
    half = nz // 2
    z, x, y, c = (lax.axis_index(a) for a in AXES)
    g = y * nc + c
    me = x * group + g
    strip = part.shape[0] // plane
    chunks = held.shape[1]
    per_device = last.shape[0]

    def member(p):
        return (z, x, p // nc, lax.rem(p, nc))

    def plane_peer(k):
        p = lax.rem(me + k, plane)
        return p, (z, p // group, lax.rem(p, group) // nc, lax.rem(p, nc))

    def ring_peer(k):
        q = lax.rem(z + k, nz)
        return q, (q, x, y, c)

    def remote(source, target, send_sem, recv_sem, device):
        return pltpu.make_async_remote_copy(
            src_ref=source,
            dst_ref=target,
            send_sem=send_sem,
            recv_sem=recv_sem,
            device_id=device,
            device_id_type=MESH,
        )

    barrier = pltpu.get_barrier_semaphore()

    def greet(peer):
        def body(k, carry):
            pl.semaphore_signal(barrier, inc=1, device_id=peer(k)[1], device_id_type=MESH)
            return carry

        return body

    lax.fori_loop(1, plane, greet(plane_peer), 0)
    lax.fori_loop(1, nz, greet(ring_peer), 0)
    load_held = pltpu.make_async_copy(bwd, held, local_sem.at[0])
    load_keep = pltpu.make_async_copy(fwd.at[:, :, c], keep, local_sem.at[1])
    load_held.start()
    load_keep.start()
    pl.semaphore_wait(barrier, plane - 1 + nz - 1)

    other = (z, x, y, nc - 1 - c)
    core_copy = remote(
        fwd.at[:, :, nc - 1 - c], from_core, plane_sent.at[0, 0], plane_came.at[0, 0], other
    )
    core_copy.start()

    d0 = lax.rem(g - z + nz, nz)
    lower = jnp.logical_and(d0 >= 1, d0 <= half)
    hu = jnp.where(lower, 0, 1)
    hd = 1 - hu
    du = jnp.where(lower, d0, lax.rem(d0 + half, nz))
    pu = half - du
    pd = du - 1
    target = du == half
    above = (lax.rem(z + 1, nz), x, y, c)
    below = (lax.rem(z + nz - 1, nz), x, y, c)

    def up(j):
        return remote(
            held.at[hu, j], from_below.at[j], chain_sent.at[0, j], chain_came.at[0, j], above
        )

    def down(j):
        return remote(
            held.at[hd, j], from_above.at[j], chain_sent.at[1, j], chain_came.at[1, j], below
        )

    def scatter(j, at):
        return remote(
            held.at[hd, j], last.at[at], last_sent.at[j], last_came.at[at], member(j // per_device)
        )

    load_held.wait()

    def step(i, carry):
        j = i - SKEW * pu

        @pl.when(jnp.logical_and(j >= 0, j < chunks))
        def _():
            @pl.when(pu > 0)
            def _():
                up(j).wait_recv()
                held[hu, j] += from_below[j]

            up(j).start()

        jd = i - SKEW * pd

        @pl.when(jnp.logical_and(jnp.logical_not(target), jnp.logical_and(jd >= 0, jd < chunks)))
        def _():
            @pl.when(pd > 0)
            def _():
                down(jd).wait_recv()
                held[hd, jd] += from_above[jd]

            down(jd).start()

        jt = i - SKEW * half

        @pl.when(jnp.logical_and(target, jnp.logical_and(jt >= 0, jt < chunks)))
        def _():
            up(jt).wait_recv()
            down(jt).wait_recv()
            held[hd, jt] += from_below[jt] + from_above[jt]
            at = lax.rem(jt, per_device)

            @pl.when(jt // per_device == g)
            def _():
                last[at] = held[hd, jt]

            @pl.when(jt // per_device != g)
            def _():
                scatter(jt, at).start()

        return carry

    steps = chunks + SKEW * half
    cut = (steps // 6, (3 * steps) // 5)
    lax.fori_loop(0, cut[0], step, 0)

    load_keep.wait()
    core_copy.wait()
    rows = keep.shape[2]
    top, low = pl.ds(0, rows // 2), pl.ds(rows // 2, rows // 2)

    def add_core(i, carry):
        at = (i // ny, lax.rem(i, ny))
        keep[at] += from_core[at]
        return carry

    lax.fori_loop(0, nx * ny, add_core, 0)

    def x_copy(k):
        p = lax.rem(x + k, nx)
        return remote(
            keep.at[p, :, top],
            from_x.at[x],
            plane_sent.at[1, k],
            plane_came.at[1, x],
            (z, p, y, c),
        )

    def y_copy(k):
        p = lax.rem(y + k, ny)
        return remote(
            keep.at[:, p, low],
            from_y.at[y],
            plane_sent.at[2, k],
            plane_came.at[2, y],
            (z, x, p, c),
        )

    for k in range(1, max(nx, ny)):
        if k < nx:
            x_copy(k).start()
        if k < ny:
            y_copy(k).start()

    lax.fori_loop(cut[0], cut[1], step, 0)

    def x_source(k):
        p = lax.rem(x + k, nx)
        return p, remote(
            from_x.at[p], from_x.at[p], plane_sent.at[1, k], plane_came.at[1, p], (z, p, y, c)
        )

    def y_source(k):
        p = lax.rem(y + k, ny)
        return p, remote(
            from_y.at[p], from_y.at[p], plane_sent.at[2, k], plane_came.at[2, p], (z, x, p, c)
        )

    for k in range(1, nx):
        p, copy = x_source(k)
        copy.wait_recv()
        keep[x, :, top] += from_x[p]
    for k in range(1, ny):
        p, copy = y_source(k)
        copy.wait_recv()
        keep[:, y, low] += from_y[p]

    def last_y(k, at):
        p = lax.rem(y + k, ny)
        return remote(
            keep.at[x, p, top],
            end_y.at[at],
            plane_sent.at[3, k],
            plane_came.at[3, at],
            (z, x, p, c),
        )

    def last_x(k, at):
        p = lax.rem(x + k, nx)
        return remote(
            keep.at[p, y, low],
            end_x.at[at],
            plane_sent.at[4, k],
            plane_came.at[4, at],
            (z, p, y, c),
        )

    for k in range(1, max(nx, ny)):
        if k < ny:
            last_y(k, y).start()
        if k < nx:
            last_x(k, x).start()

    lax.fori_loop(cut[1], steps, step, 0)

    upper = keep[x, y, top]
    for k in range(1, ny):
        p = lax.rem(y + k, ny)
        last_y(k, p).wait_recv()
        upper = upper + end_y[p]
    lower_rows = keep[x, y, low]
    for k in range(1, nx):
        p = lax.rem(x + k, nx)
        last_x(k, p).wait_recv()
        lower_rows = lower_rows + end_x[p]
    total = jnp.concatenate([upper, lower_rows], axis=0)
    holder = lax.rem(z, group)

    @pl.when(holder != g)
    def _():
        for at in range(per_device):
            scatter(at, at).wait_recv()

    total = total + last[...].reshape(total.shape)
    product[...] = total
    part[...] = lax.dot_general(
        total, total, (((0,), (0,)), ((), ())), precision=HIGHEST, preferred_element_type=jnp.float32
    )

    def rows_of(p):
        return pl.ds(pl.multiple_of(p * strip, strip), strip)

    def exchange(count, peer, stage, mine, source, target_of):
        def copy(k, p, device):
            return remote(
                source(p), target_of(mine), sent.at[stage, k], came.at[stage, mine], device
            )

        def start(k, carry):
            p, device = peer(k)
            copy(k, p, device).start()
            return carry

        def finish(k, carry):
            p, device = peer(k)
            remote(
                target_of(p), target_of(p), sent.at[stage, k], came.at[stage, p], device
            ).wait_recv()
            return carry

        def left(k, carry):
            p, device = peer(k)
            copy(k, p, device).wait_send()
            return carry

        lax.fori_loop(1, count, start, 0)
        lax.fori_loop(1, count, finish, 0)
        return lambda: lax.fori_loop(1, count, left, 0)

    left_first = exchange(plane, plane_peer, 0, me, lambda p: part.at[rows_of(p)], lambda p: got.at[p])
    strip_sum = part[rows_of(me)]
    for k in range(1, plane):
        strip_sum = strip_sum + got[lax.rem(me + k, plane)]
    ring[z] = strip_sum
    left_ring = exchange(nz, ring_peer, 1, z, lambda p: ring.at[z], lambda p: ring.at[p])
    strip_sum = ring[0]
    for k in range(1, nz):
        strip_sum = strip_sum + ring[k]
    whole[rows_of(me)] = strip_sum
    left_last = exchange(
        plane, plane_peer, 2, me, lambda p: whole.at[rows_of(me)], lambda p: whole.at[rows_of(p)]
    )
    gram[...] = whole[...]

    left_first()
    left_ring()
    left_last()
    for k in range(1, nx):
        x_copy(k).wait_send()
        last_x(k, x).wait_send()
    for k in range(1, ny):
        y_copy(k).wait_send()
        last_y(k, y).wait_send()

    def drain(j, carry):
        up(j).wait_send()

        @pl.when(jnp.logical_not(target))
        def _():
            down(j).wait_send()

        @pl.when(jnp.logical_and(target, j // per_device != g))
        def _():
            scatter(j, lax.rem(j, per_device)).wait_send()

        return carry

    lax.fori_loop(0, chunks, drain, 0)


def device_sums(fwd, bwd):
    sizes = axis_sizes()
    nz, nx, ny, nc = sizes
    group = ny * nc
    plane = nx * group
    _, rows, width = fwd.shape
    strip = width // plane
    most = max(plane, nz)
    chunks = group * rows // CHUNK
    fwd = fwd.reshape(nx, ny, nc, rows, width)
    bwd = bwd.reshape(2, chunks, CHUNK, width)
    vmem = pl.BlockSpec(memory_space=pltpu.VMEM)
    anywhere = pl.BlockSpec(memory_space=pl.ANY)

    def buffer(*shape):
        return pltpu.VMEM(shape, jnp.float32)

    dma = pltpu.SemaphoreType.DMA
    return pl.pallas_call(
        functools.partial(sums_kernel, sizes),
        out_shape=[
            jax.ShapeDtypeStruct((rows, width), jnp.float32),
            jax.ShapeDtypeStruct((width, width), jnp.float32),
        ],
        in_specs=[anywhere, anywhere],
        out_specs=[vmem, vmem],
        scratch_shapes=[
            buffer(2, chunks, CHUNK, width),
            buffer(nx, ny, rows, width),
            buffer(nx, ny, rows, width),
            buffer(nx, ny, rows // 2, width),
            buffer(ny, nx, rows // 2, width),
            buffer(nx, rows // 2, width),
            buffer(ny, rows // 2, width),
            buffer(chunks, CHUNK, width),
            buffer(chunks, CHUNK, width),
            buffer(rows // CHUNK, CHUNK, width),
            buffer(width, width),
            buffer(plane, strip, width),
            buffer(nz, strip, width),
            buffer(width, width),
            dma((2,)),
            dma((2, chunks)),
            dma((2, chunks)),
            dma((chunks,)),
            dma((rows // CHUNK,)),
            dma((5, max(nx, ny))),
            dma((5, max(nx, ny))),
            dma((3, most)),
            dma((3, most)),
        ],
        compiler_params=pltpu.CompilerParams(
            collective_id=0, has_side_effects=True, vmem_limit_bytes=VMEM_LIMIT
        ),
        name="device_sums",
    )(fwd, bwd)


def dot_high(a, b, dims):
    return lax.dot_general(
        a, b, (dims, ((), ())), precision=HIGHEST, preferred_element_type=jnp.float32
    )


def inverse_factor(a):
    n = a.shape[0]
    sub = 8
    lanes = lax.broadcasted_iota(jnp.int32, (sub, n), 1)
    subs = lax.broadcasted_iota(jnp.int32, (sub, n), 0)
    left = [a[i * sub : (i + 1) * sub] for i in range(n // sub)]
    right = [(lanes == subs + i * sub).astype(jnp.float32) for i in range(n // sub)]
    for j in range(n):
        t0, s = divmod(j, sub)
        row = left[t0][s : s + 1]
        inv = 1.0 / row[:, j : j + 1]
        wrow = right[t0][s : s + 1]
        scaled = row * inv
        wscaled = wrow * inv
        for t in range(t0, n // sub):
            col = left[t][:, j : j + 1]
            if t == t0:
                col = jnp.where(subs[:, :1] > s, col, 0.0)
            left[t] = left[t] - col * scaled
            right[t] = right[t] - col * wscaled
    out = []
    for t in range(n // sub):
        d = jnp.sum(jnp.where(lanes == subs + t * sub, left[t], 0.0), axis=1, keepdims=True)
        out.append(right[t] * lax.rsqrt(d))
    return jnp.concatenate(out, axis=0)


def eliminated(gram, scale, inverse):
    h = gram.shape[0] // 2
    g21 = gram[h:, :h] * scale
    w11 = inverse_factor(gram[:h, :h] * scale)
    l21 = dot_high(g21, w11, ((1,), (1,)))
    w22 = inverse_factor(gram[h:, h:] * scale - dot_high(l21, l21, ((1,), (1,))))
    inverse[:h, :h] = w11
    inverse[:h, h:] = jnp.zeros((h, h), jnp.float32)
    inverse[h:, :h] = -dot_high(w22, dot_high(l21, w11, ((1,), (0,))), ((1,), (0,)))
    inverse[h:, h:] = w22


def basis_kernel(scale, gram, product, basis, inverse):
    n = gram.shape[0]
    line = lax.broadcasted_iota(jnp.int32, (n, n), 0)
    lane = lax.broadcasted_iota(jnp.int32, (n, n), 1)
    one = (line == lane).astype(jnp.float32)
    weight = jnp.where(line > lane, 1.0, 0.5 * one)
    g = gram[...] * scale
    d_line = lax.rsqrt(jnp.sum(g * one, axis=1, keepdims=True))
    d_lane = lax.rsqrt(jnp.sum(g * one, axis=0, keepdims=True))
    w = (one - weight * (g * d_line * d_lane - one)) * d_lane
    for turn in range(2):
        off = dot_high(dot_high(w, g, ((1,), (0,))), w, ((1,), (1,))) - one
        w = w - dot_high(weight * off, w, ((1,), (0,)))
    inverse[...] = w
    settled = jnp.sum(off * off) < 1e-6

    @pl.when(jnp.logical_not(settled))
    def _():
        eliminated(gram, scale, inverse)

    basis[...] = dot_high(product[...], inverse[...], ((1,), (1,)))


def new_basis(gram, product, nodes):
    vmem = pl.BlockSpec(memory_space=pltpu.VMEM)
    return pl.pallas_call(
        functools.partial(basis_kernel, 1.0 / nodes),
        out_shape=jax.ShapeDtypeStruct(product.shape, jnp.float32),
        in_specs=[vmem, vmem],
        out_specs=vmem,
        scratch_shapes=[pltpu.VMEM(gram.shape, jnp.float32)],
        compiler_params=pltpu.CompilerParams(vmem_limit_bytes=VMEM_LIMIT),
        name="new_basis",
    )(gram, product)


def shards(panel, lists, tiles):
    nz, nx, ny, nc = axis_sizes()
    group = ny * nc
    plane = nx * group
    tile = tiles.shape[1]
    width = panel.shape[1]
    blocks = panel.shape[0] // tile
    nodes = panel.shape[0] * nz * plane
    his = nz // group
    own = panel.reshape(blocks, tile, width)
    entries = lists.reshape(3, his, group, nx).transpose(3, 2, 1, 0).reshape(plane, 1, 3 * his)
    entries = jnp.pad(entries.astype(jnp.float32), ((0, 0), (his, 7 - his), (0, 128 - 3 * his)))
    here, meta, cols, rows = bring(own, entries, tiles.reshape(his, group * nx, tile, tile))
    rows = rows.reshape(plane, blocks, tile, width)
    picks = meta[:, his, : 3 * his].astype(jnp.int32).reshape(plane * his, 3).T
    fwd, bwd = tile_products(picks, here, meta, cols, rows)
    product, gram = device_sums(
        fwd.reshape(plane, blocks * tile, width), bwd.reshape(his, group * blocks * tile, width)
    )
    return new_basis(gram, product, nodes)


def solution(mesh):
    sizes = mesh.devices.shape
    nx, ny, nc = grid_of(sizes)
    fine = Mesh(mesh.devices.reshape(sizes[0] // nx, nx, ny, nc), AXES)
    return jax.shard_map(
        shards,
        mesh=fine,
        in_specs=(P(AXES, None), P(None, AXES), P(AXES, None, None)),
        out_specs=P(AXES, None),
        check_vma=False,
    )


def grid_of(sizes):
    return (4, 4, 2) if sizes == (64, 8) else (2, 1, 2)
```
